768 devices in a mesh: sec: 16 (over y, core), grp: 48 (over x, z).
Axes of the slice: x: 4, y: 8, z: 12, core: 2. Of those that a mesh axis runs over, the one named last changes fastest.
Arguments:
- positions: float32 [3, 393216], P(None, ('sec', 'grp')), may hold values from -9 to 9, as said below
- velocities: float32 [3, 393216], P(None, ('sec', 'grp')), may hold values from -4 to 4
- masses: float32 [393216], P(('sec', 'grp')), may hold values from 0.004 to 0.04
- near_list: int32 [1536, 64], P(('sec', 'grp')), may hold values from 0 to 31, as said below
- near_count: int32 [1536], P(('sec', 'grp')), may hold values from 1 to 64, as said below
- far_list: int32 [1536, 32], P(('sec', 'grp')), may hold values from 0 to 1535
Outputs:
- positions_out: float32 [3, 393216], P(None, ('sec', 'grp'))
- velocities_out: float32 [3, 393216], P(None, ('sec', 'grp'))
- accel_out: float32 [3, 393216], P(None, ('sec', 'grp'))
The draws below stay inside these ranges and needn't reach their ends.
Inputs may be any that keep to these rules, and one draw needn't show every extreme that they name: `positions`: within the range stated, particles of a block lie near one another and blocks of a group near their group. `near_list`: numbers within the group: the section index times 2 plus the block's place on its device. Slot 0 names the block itself. `near_count`: some block has all 64 slots used.
All inputs are finite; a program needn't handle non-finite values.
Results may differ from the reference program's by a relative error of at most 0.0001.
Values sent between devices are 32-bit elements; how exact they have to be, the bound alone decides.
No kernel may reach another device: no remote copies, remote signals or barrier semaphores. Data moves between devices by JAX's collectives and lax.ppermute only.
A program may use at most 32 MiB of HBM per device.

```python
import math
import jax
import jax.numpy as jnp
from jax import lax

B = 256
NB_DEV = 2
LIST = 64
FAR = 32
GBLK = 32
NBLK = 1536
NPART = 393216
N_GRP = 48


def draw_positions(key, part):
    first, second, third = jax.random.split(key, 3)
    groups = NBLK // GBLK
    centres = jax.random.uniform(first, (3, groups), jnp.float32, -4.0, 4.0)
    block_ids = jnp.arange(NBLK)
    group_of = block_ids // NB_DEV % groups
    block_centre = centres[:, group_of] + jax.random.uniform(second, (3, NBLK), jnp.float32, -1.5, 1.5)
    offsets = jnp.clip(0.6 * jax.random.normal(third, (3, NBLK, B), jnp.float32), -3.0, 3.0)
    return (block_centre[:, :, None] + offsets).reshape(3, NBLK * B)


def draw_near_list(key, part):
    groups = NBLK // GBLK
    block_ids = jnp.arange(NBLK, dtype=jnp.int32)
    section = block_ids // (NB_DEV * groups)
    own = section * NB_DEV + block_ids % NB_DEV
    listed = jax.random.randint(key, (NBLK, LIST), 0, GBLK, jnp.int32)
    return listed.at[:, 0].set(own)


def draw_near_count(key, part):
    first, second = jax.random.split(jax.random.fold_in(key, 7))
    devices = NBLK // NB_DEV
    level = jax.random.randint(first, (devices,), 0, 3, jnp.int32).at[0].set(0)
    most = LIST // jnp.left_shift(jnp.int32(1), level)
    block_ids = jnp.arange(NBLK, dtype=jnp.int32)
    device_of = block_ids // NB_DEV
    counts = jax.random.randint(second, (NBLK,), 1, most[device_of] + 1, jnp.int32)
    return jnp.where(block_ids % NB_DEV == 0, most[device_of], counts).astype(jnp.int32)


def plant(entries, key, smallest, high):
    longest = entries.shape.index(max(entries.shape))
    spots = []
    for shift in (0, 1):
        where = [jax.random.randint(jax.random.fold_in(key, axis), (), 0, length) for axis, length in enumerate(entries.shape)]
        where[longest] = (where[longest] + shift) % entries.shape[longest]
        spots.append(tuple(where))
    return entries.at[spots[0]].set(smallest).at[spots[1]].set(high)


def level_of(key, dims, pieces, low, top_value):
    gain, own = 1.0, jax.random.fold_in(key, 6)
    for position, shards_of in pieces:
        heights = jnp.exp(jax.random.uniform(jax.random.fold_in(own, position), (shards_of,), jnp.float32, low / len(pieces), top_value / len(pieces)))
        gain = gain * jnp.repeat(heights, dims[position] // shards_of).reshape([-1 if axis == position else 1 for axis in range(len(dims))])
    return gain


def centred(stream_key, shape, width, most, cuts=(), held_as=jnp.bfloat16):
    loudness = level_of(stream_key, shape, cuts, -0.22, 0.18) if cuts else 1.0
    values = jax.random.normal(stream_key, shape, jnp.float32) * width * loudness
    return jnp.minimum(jnp.maximum(values, -most), most).astype(held_as)


def setup_inputs(seed: int = 0) -> dict:
    keys = jax.random.split(jax.random.key(seed), 7)
    return {
        "positions": draw_positions(jax.random.fold_in(keys[6], 71), 0),
        "velocities": centred(keys[1], (3, NPART), 1.0, 4.0, ((1, 768),), jnp.float32),
        "masses": jnp.clip(jnp.exp(math.log(0.04) - 2.30258502 * jax.random.uniform(keys[2], (NPART,), jnp.float32) ** level_of(keys[2], (NPART,), ((0, 768),), -0.2, 0.2)), 0.004, 0.04),
        "near_list": draw_near_list(jax.random.fold_in(keys[6], 71), 0),
        "near_count": draw_near_count(jax.random.fold_in(keys[6], 71), 0),
        "far_list": plant(jax.random.randint(keys[5], (NBLK, FAR), 0, NBLK), jax.random.fold_in(keys[5], 1), 0, NBLK - 1).astype(jnp.int32),
    }


timestep = 0.05
softening = 0.25

def pair_accel(target, source):
    delta_x = source[0][:, None, :] - target[0][:, :, None]
    delta_y = source[1][:, None, :] - target[1][:, :, None]
    delta_z = source[2][:, None, :] - target[2][:, :, None]
    square = delta_x * delta_x + delta_y * delta_y + delta_z * delta_z + softening
    weight = source[3][:, None, :] / (square * jnp.sqrt(square))
    return jnp.stack([lax.optimization_barrier(jnp.sum(weight * delta_x, -1)), lax.optimization_barrier(jnp.sum(weight * delta_y, -1)), lax.optimization_barrier(jnp.sum(weight * delta_z, -1))])

def far_accel(target, moment):
    rel_x = target[0][:, None, :] - moment[1][:, :, None]
    rel_y = target[1][:, None, :] - moment[2][:, :, None]
    rel_z = target[2][:, None, :] - moment[3][:, :, None]
    square = rel_x * rel_x + rel_y * rel_y + rel_z * rel_z + softening
    inv_three = 1.0 / (square * jnp.sqrt(square))
    inv_five = inv_three / square
    inv_seven = inv_five / square
    quad_x = moment[4][..., None] * rel_x + moment[7][..., None] * rel_y + moment[8][..., None] * rel_z
    quad_y = moment[7][..., None] * rel_x + moment[5][..., None] * rel_y + moment[9][..., None] * rel_z
    quad_z = moment[8][..., None] * rel_x + moment[9][..., None] * rel_y + moment[6][..., None] * rel_z
    inner = rel_x * quad_x + rel_y * quad_y + rel_z * quad_z
    mass = moment[0][..., None]
    acc_x = lax.optimization_barrier(jnp.sum(-mass * rel_x * inv_three - quad_x * inv_five + 2.5 * inner * rel_x * inv_seven, 1))
    acc_y = lax.optimization_barrier(jnp.sum(-mass * rel_y * inv_three - quad_y * inv_five + 2.5 * inner * rel_y * inv_seven, 1))
    acc_z = lax.optimization_barrier(jnp.sum(-mass * rel_z * inv_three - quad_z * inv_five + 2.5 * inner * rel_z * inv_seven, 1))
    return jnp.stack([acc_x, acc_y, acc_z])

def block_moments(blocks):
    weight = blocks[3]
    mass = lax.optimization_barrier(jnp.sum(weight, -1))
    centre_x = lax.optimization_barrier(jnp.sum(weight * blocks[0], -1)) / mass
    centre_y = lax.optimization_barrier(jnp.sum(weight * blocks[1], -1)) / mass
    centre_z = lax.optimization_barrier(jnp.sum(weight * blocks[2], -1)) / mass
    off_x = blocks[0] - centre_x[:, None]
    off_y = blocks[1] - centre_y[:, None]
    off_z = blocks[2] - centre_z[:, None]
    radius = off_x * off_x + off_y * off_y + off_z * off_z
    return jnp.stack([mass, centre_x, centre_y, centre_z, lax.optimization_barrier(jnp.sum(weight * (3.0 * off_x * off_x - radius), -1)), lax.optimization_barrier(jnp.sum(weight * (3.0 * off_y * off_y - radius), -1)), lax.optimization_barrier(jnp.sum(weight * (3.0 * off_z * off_z - radius), -1)), lax.optimization_barrier(jnp.sum(3.0 * weight * off_x * off_y, -1)), lax.optimization_barrier(jnp.sum(3.0 * weight * off_x * off_z, -1)), lax.optimization_barrier(jnp.sum(3.0 * weight * off_y * off_z, -1))])

def accelerate(half, masses, global_near, near_count, far_list):
    blocks = jnp.concatenate([half, masses[None, :]], 0).reshape(4, NBLK, B)
    moments = block_moments(blocks)

    def one_block(index):
        target = blocks[:3, index][:, None, :]

        def add_slot(slot, total):
            source = blocks[:, global_near[index, slot]][:, None, :]
            return total + pair_accel(target, source)
        direct = lax.fori_loop(0, near_count[index], add_slot, jnp.zeros((3, 1, B), jnp.float32))
        far = far_accel(target, moments[:, far_list[index]][:, None, :])
        return (direct + far)[:, 0, :]
    result = lax.map(one_block, jnp.arange(NBLK, dtype=jnp.int32))
    return jnp.transpose(result, (1, 0, 2)).reshape(3, NBLK * B)

def reference(positions, velocities, masses, near_list, near_count, far_list):
    block_ids = jnp.arange(NBLK, dtype=jnp.int32)
    group_of = block_ids // NB_DEV % N_GRP
    section = near_list // NB_DEV
    place = near_list % NB_DEV
    global_near = ((section * N_GRP + group_of[:, None]) * NB_DEV + place).astype(jnp.int32)
    current = positions
    speed = velocities
    accel = jnp.zeros_like(positions)
    for step in range(2):
        half = current + 0.5 * timestep * speed
        accel = accelerate(half, masses, global_near, near_count, far_list)
        speed = speed + timestep * accel
        current = half + 0.5 * timestep * speed
    return (current, speed, accel)
```

```python
import jax
import jax.numpy as jnp
from jax import lax
from jax.experimental import pallas as pl
from jax.experimental.pallas import tpu as pltpu
from jax.sharding import PartitionSpec as P

timestep = 0.05
softening = 0.25
N_SEC = 16
N_GRP = 48
B = 256
W = 2 * B
KBLK = 2 * N_SEC
LIST = 64
FAR = 32
CHUNK = 1024
f32 = jnp.float32
bf16 = jnp.bfloat16
VMEM = pl.BlockSpec(memory_space=pltpu.VMEM)
SMEM = pl.BlockSpec(memory_space=pltpu.SMEM)
PARAMS = pltpu.CompilerParams(vmem_limit_bytes=40 * 1024 * 1024)


def shape(*dims):
    return jax.ShapeDtypeStruct(dims, f32)


def split3(value):
    first = value.astype(bf16).astype(f32)
    rest = value - first
    second = rest.astype(bf16).astype(f32)
    return first, second, rest - second


def opening(pos_ref, vel_ref, mass_ref, near_ref, count_ref, send_ref, own_ref, times_ref):
    half = pos_ref[...] + (0.5 * timestep) * vel_ref[...]
    own = jnp.concatenate([half, mass_ref[...]], 0)
    own_ref[...] = own
    for d in range(N_SEC):
        send_ref[d] = own
    block = lax.broadcasted_iota(jnp.int32, (KBLK, LIST), 0)
    slot = lax.broadcasted_iota(jnp.int32, (KBLK, LIST), 1)
    for b in range(2):
        hit = (near_ref[b : b + 1, :] == block) & (slot < count_ref[b])
        times = jnp.sum(jnp.where(hit, 1.0, 0.0).astype(f32), axis=1, keepdims=True)
        times_ref[b] = jnp.broadcast_to(times, (KBLK, 128))


def group_moments(ghost_ref, out_ref):
    section = lax.broadcasted_iota(jnp.int32, (N_SEC, 128), 0)
    lane = lax.broadcasted_iota(jnp.int32, (N_SEC, 128), 1)
    base = section // 4 * 32
    packed = jnp.zeros((N_SEC, 128), f32)
    whole = [ghost_ref[:, c, :] for c in range(4)]

    def total(v):
        return jnp.sum(v, axis=1, keepdims=True)

    for place in range(2):
        x, y, z, m = [w[:, B * place : B * place + B] for w in whole]
        mass = total(m)
        centre = [total(m * v) / mass for v in (x, y, z)]
        dx, dy, dz = [v - c for v, c in zip((x, y, z), centre)]
        radius = dx * dx + dy * dy + dz * dz
        m3 = 3.0 * m
        numbers = [
            mass,
            *centre,
            total(m * (3.0 * dx * dx - radius)),
            total(m * (3.0 * dy * dy - radius)),
            total(m * (3.0 * dz * dz - radius)),
            total(m3 * dx * dy),
            total(m3 * dx * dz),
            total(m3 * dy * dz),
        ]
        for c, number in enumerate(numbers):
            packed = jnp.where(lane == base + (16 * place + c), number, packed)
    message = packed[0:4] + packed[4:8] + packed[8:12] + packed[12:16]
    for k in range(N_GRP):
        out_ref[k] = message


def direct(own_ref, ghost_ref, times_ref, out_ref, source_ref, weight_ref, total_ref):
    tot = ghost_ref[0]
    for d in range(1, N_SEC):
        tot = tot + ghost_ref[d]
    middle = jnp.sum(tot, axis=1, keepdims=True)[0:3] * (1.0 / (N_SEC * W))
    target = own_ref[0:3, :] - middle
    norm = jnp.sum(target * target, axis=0, keepdims=True) + softening
    pad = jnp.zeros((3, W), f32)
    a, b, c = split3(jnp.concatenate([-2.0 * target, jnp.ones((1, W), f32), norm, pad], 0))
    targets = jnp.concatenate([a, a, a, b, b, c], 0).astype(bf16)
    for d in range(N_SEC):
        ghost = ghost_ref[d]
        source = ghost[0:3] - middle
        mass = ghost[3:4]
        square = jnp.sum(source * source, axis=0, keepdims=True)
        a, b, c = split3(jnp.concatenate([source, square, jnp.ones((1, W), f32), pad], 0))
        source_ref[:, W * d : W * d + W] = jnp.concatenate([a, b, c, a, b, a], 0).astype(bf16)
        terms = jnp.concatenate([mass, source * mass], 0)
        both = []
        for t in range(2):
            first, second = times_ref[t, 2 * d : 2 * d + 1, :], times_ref[t, 2 * d + 1 : 2 * d + 2, :]
            both.append(terms * jnp.concatenate([first, first, second, second], 1))
        a, b, c = split3(jnp.concatenate(both, 0))
        weight_ref[:, W * d : W * d + W] = jnp.concatenate([a, b, c, jnp.zeros_like(a)], 0).astype(bf16)
    total_ref[...] = jnp.zeros_like(total_ref)

    @pl.loop(0, N_SEC * W // CHUNK, unroll=2)
    def _(step):
        at = pl.ds(pl.multiple_of(step * CHUNK, CHUNK), CHUNK)
        square = lax.dot_general(
            source_ref[:, at], targets, (((0,), (0,)), ((), ())), preferred_element_type=f32
        )
        inverse = lax.rsqrt(square)
        cube = inverse * inverse * inverse
        high = cube.astype(bf16)
        low = (cube - high.astype(f32)).astype(bf16)
        weight = weight_ref[:, at]
        total_ref[...] += jnp.dot(weight, high, preferred_element_type=f32) + jnp.dot(
            weight, low, preferred_element_type=f32
        )

    sums = total_ref[0:8] + total_ref[8:16] + total_ref[16:24]
    lane = lax.broadcasted_iota(jnp.int32, (4, W), 1)
    sums = jnp.where(lane < B, sums[0:4], sums[4:8])
    out_ref[...] = sums[1:4] - target * sums[0:1]


def far_field(own_ref, moments_ref, far_ref, picked_ref):
    for b in range(2):
        for e in range(FAR):
            block = far_ref[b, e]
            device = block // 2
            place = block - device * 2
            section = device // N_GRP
            group = device - section * N_GRP
            high = section // 4
            row = group * 4 + (section - high * 4)
            shift = (128 - (high * 32 + place * 16)) % 128
            line = moments_ref[pl.ds(row, 1), :]
            picked_ref[b * FAR + e : b * FAR + e + 1, :] = pltpu.roll(line, shift, 1)
    out = []
    for b in range(2):
        picked = picked_ref[FAR * b : FAR * b + FAR, :]
        mass, cx, cy, cz, qxx, qyy, qzz, qxy, qxz, qyz = [picked[:, c : c + 1] for c in range(10)]
        x, y, z = [own_ref[c : c + 1, B * b : B * b + B] for c in range(3)]
        x, y, z = x - cx, y - cy, z - cz
        square = x * x + y * y + z * z + softening
        inverse = lax.rsqrt(square)
        two = inverse * inverse
        three = inverse * two
        five = three * two
        seven = five * two
        quad_x = qxx * x + qxy * y + qxz * z
        quad_y = qxy * x + qyy * y + qyz * z
        quad_z = qxz * x + qyz * y + qzz * z
        along = 2.5 * (x * quad_x + y * quad_y + z * quad_z) * seven - mass * three
        out.append(
            jnp.concatenate(
                [
                    jnp.sum(along * r - quad * five, axis=0, keepdims=True)
                    for r, quad in ((x, quad_x), (y, quad_y), (z, quad_z))
                ],
                0,
            )
        )
    return jnp.concatenate(out, 1)


def first_step(own_ref, vel_ref, direct_ref, moments_ref, far_ref, send_ref, next_ref, speed_ref, picked_ref):
    accel = direct_ref[...] + far_field(own_ref, moments_ref, far_ref, picked_ref)
    speed = vel_ref[...] + timestep * accel
    speed_ref[...] = speed
    current = own_ref[0:3, :] + (0.5 * timestep) * speed
    half = current + (0.5 * timestep) * speed
    own = jnp.concatenate([half, own_ref[3:4, :]], 0)
    next_ref[...] = own
    for d in range(N_SEC):
        send_ref[d] = own


def last_step(own_ref, vel_ref, direct_ref, moments_ref, far_ref, pos_ref, speed_ref, accel_ref, picked_ref):
    accel = direct_ref[...] + far_field(own_ref, moments_ref, far_ref, picked_ref)
    accel_ref[...] = accel
    speed = vel_ref[...] + timestep * accel
    speed_ref[...] = speed
    pos_ref[...] = own_ref[0:3, :] + (0.5 * timestep) * speed


def on_device(positions, velocities, masses, near_list, near_count, far_list):
    send, own, times = pl.pallas_call(
        opening,
        out_shape=(shape(N_SEC, 4, W), shape(4, W), shape(2, KBLK, 128)),
        in_specs=[VMEM, VMEM, VMEM, VMEM, SMEM],
        out_specs=(VMEM, VMEM, VMEM),
        compiler_params=PARAMS,
    )(positions, velocities, masses.reshape(1, W), near_list, near_count)
    speed = velocities
    for step in range(2):
        ghosts = lax.all_to_all(send, "sec", split_axis=0, concat_axis=0, tiled=True)
        message = pl.pallas_call(
            group_moments,
            out_shape=shape(N_GRP, 4, 128),
            in_specs=[VMEM],
            out_specs=VMEM,
            compiler_params=PARAMS,
        )(ghosts)
        moments = lax.all_to_all(message, "grp", split_axis=0, concat_axis=0, tiled=True)
        near = pl.pallas_call(
            direct,
            out_shape=shape(3, W),
            in_specs=[VMEM] * 3,
            out_specs=VMEM,
            scratch_shapes=[
                pltpu.VMEM((48, N_SEC * W), bf16),
                pltpu.VMEM((32, N_SEC * W), bf16),
                pltpu.VMEM((32, W), f32),
            ],
            compiler_params=PARAMS,
            cost_estimate=pl.CostEstimate(
                flops=2 * 80 * W * N_SEC * W, bytes_accessed=200000, transcendentals=W * N_SEC * W
            ),
        )(own, ghosts, times)
        last = step == 1
        made = pl.pallas_call(
            last_step if last else first_step,
            out_shape=(shape(3, W),) * 3 if last else (shape(N_SEC, 4, W), shape(4, W), shape(3, W)),
            in_specs=[VMEM, VMEM, VMEM, VMEM, SMEM],
            out_specs=(VMEM,) * 3,
            scratch_shapes=[pltpu.VMEM((2 * FAR, 128), f32)],
            compiler_params=PARAMS,
        )(own, speed, near, moments.reshape(N_GRP * 4, 128), far_list)
        if last:
            return made
        send, own, speed = made


def solution(mesh):
    placed = (
        P(None, ("sec", "grp")),
        P(None, ("sec", "grp")),
        P(("sec", "grp")),
        P(("sec", "grp"), None),
        P(("sec", "grp")),
        P(("sec", "grp"), None),
    )
    return jax.shard_map(
        on_device,
        mesh=mesh,
        in_specs=placed,
        out_specs=(P(None, ("sec", "grp")), P(None, ("sec", "grp")), P(None, ("sec", "grp"))),
        check_vma=False,
    )
```

```python
import jax
import jax.numpy as jnp
from jax import lax
from jax.experimental import pallas as pl
from jax.experimental.pallas import tpu as pltpu
from jax.sharding import PartitionSpec as P

timestep = 0.05
softening = 0.25
N_Y = 8
N_SEC = 16
N_GRP = 48
B = 256
W = 2 * B
KBLK = 2 * N_SEC
LIST = 64
FAR = 32
CHUNK = 1024
f32 = jnp.float32
bf16 = jnp.bfloat16
VMEM = pl.BlockSpec(memory_space=pltpu.VMEM)
SMEM = pl.BlockSpec(memory_space=pltpu.SMEM)
WHOLE = pltpu.CompilerParams(vmem_limit_bytes=62 * 1024 * 1024)
PARAMS = pltpu.CompilerParams(vmem_limit_bytes=40 * 1024 * 1024)


def shape(*dims):
    return jax.ShapeDtypeStruct(dims, f32)


def split3(value):
    first = value.astype(bf16).astype(f32)
    rest = value - first
    second = rest.astype(bf16).astype(f32)
    return first, second, rest - second


def opening(pos_hbm, vel_hbm, mass_hbm, send_ref, own_ref, pos_ref, vel_ref, mass_ref, sems):
    copies = [
        pltpu.make_async_copy(source, target, sems.at[i])
        for i, (source, target) in enumerate(((pos_hbm, pos_ref), (vel_hbm, vel_ref), (mass_hbm, mass_ref)))
    ]
    for copy in copies:
        copy.start()
    for copy in copies:
        copy.wait()
    half = pos_ref[...] + (0.5 * timestep) * vel_ref[...]
    own = jnp.concatenate([half, mass_ref[...]], 0)
    own_ref[...] = own
    for d in range(N_Y):
        send_ref[d] = own


def group_moments(ghost_ref, out_ref):
    section = lax.broadcasted_iota(jnp.int32, (N_SEC, 128), 0)
    lane = lax.broadcasted_iota(jnp.int32, (N_SEC, 128), 1)
    base = section // 4 * 32
    packed = jnp.zeros((N_SEC, 128), f32)
    whole = [ghost_ref[:, c, :] for c in range(4)]

    def total(v):
        return jnp.sum(v, axis=1, keepdims=True)

    for place in range(2):
        x, y, z, m = [w[:, B * place : B * place + B] for w in whole]
        mass = total(m)
        centre = [total(m * v) / mass for v in (x, y, z)]
        dx, dy, dz = [v - c for v, c in zip((x, y, z), centre)]
        radius = dx * dx + dy * dy + dz * dz
        m3 = 3.0 * m
        numbers = [
            mass,
            *centre,
            total(m * (3.0 * dx * dx - radius)),
            total(m * (3.0 * dy * dy - radius)),
            total(m * (3.0 * dz * dz - radius)),
            total(m3 * dx * dy),
            total(m3 * dx * dz),
            total(m3 * dy * dz),
        ]
        for c, number in enumerate(numbers):
            packed = jnp.where(lane == base + (16 * place + c), number, packed)
    message = packed[0:4] + packed[4:8] + packed[8:12] + packed[12:16]
    for k in range(N_GRP):
        out_ref[k] = message


def direct(own_ref, ghost_ref, near_ref, count_ref, out_ref, source_ref, weight_ref, total_ref, times_ref):
    block = lax.broadcasted_iota(jnp.int32, (KBLK, LIST), 0)
    slot = lax.broadcasted_iota(jnp.int32, (KBLK, LIST), 1)
    for b in range(2):
        hit = (near_ref[b : b + 1, :] == block) & (slot < count_ref[b])
        times = jnp.sum(jnp.where(hit, 1.0, 0.0).astype(f32), axis=1, keepdims=True)
        times_ref[b] = jnp.broadcast_to(times, (KBLK, 128))
    tot = ghost_ref[0]
    for d in range(1, N_SEC):
        tot = tot + ghost_ref[d]
    middle = jnp.sum(tot, axis=1, keepdims=True)[0:3] * (1.0 / (N_SEC * W))
    target = own_ref[0:3, :] - middle
    norm = jnp.sum(target * target, axis=0, keepdims=True) + softening
    pad = jnp.zeros((3, W), f32)
    a, b, c = split3(jnp.concatenate([-2.0 * target, jnp.ones((1, W), f32), norm, pad], 0))
    targets = jnp.concatenate([a, a, a, b, b, c], 0).astype(bf16)
    for d in range(N_SEC):
        ghost = ghost_ref[d]
        source = ghost[0:3] - middle
        mass = ghost[3:4]
        square = jnp.sum(source * source, axis=0, keepdims=True)
        a, b, c = split3(jnp.concatenate([source, square, jnp.ones((1, W), f32), pad], 0))
        source_ref[:, W * d : W * d + W] = jnp.concatenate([a, b, c, a, b, a], 0).astype(bf16)
        terms = jnp.concatenate([mass, source * mass], 0)
        k = (d % N_Y * 2 + d // N_Y) * 2
        both = []
        for t in range(2):
            first, second = times_ref[t, k : k + 1, :], times_ref[t, k + 1 : k + 2, :]
            both.append(terms * jnp.concatenate([first, first, second, second], 1))
        a, b, c = split3(jnp.concatenate(both, 0))
        weight_ref[:, W * d : W * d + W] = jnp.concatenate([a, b, c, jnp.zeros_like(a)], 0).astype(bf16)
    total_ref[...] = jnp.zeros_like(total_ref)

    @pl.loop(0, N_SEC * W // CHUNK, unroll=2)
    def _(step):
        at = pl.ds(pl.multiple_of(step * CHUNK, CHUNK), CHUNK)
        square = lax.dot_general(
            source_ref[:, at], targets, (((0,), (0,)), ((), ())), preferred_element_type=f32
        )
        inverse = lax.rsqrt(square)
        cube = inverse * inverse * inverse
        high = cube.astype(bf16)
        low = (cube - high.astype(f32)).astype(bf16)
        weight = weight_ref[:, at]
        total_ref[...] += jnp.dot(weight, high, preferred_element_type=f32) + jnp.dot(
            weight, low, preferred_element_type=f32
        )

    sums = total_ref[0:8] + total_ref[8:16] + total_ref[16:24]
    lane = lax.broadcasted_iota(jnp.int32, (4, W), 1)
    sums = jnp.where(lane < B, sums[0:4], sums[4:8])
    out_ref[...] = sums[1:4] - target * sums[0:1]


def far_field(own_ref, moments_ref, far_ref, picked_ref):
    for b in range(2):
        for e in range(FAR):
            block = far_ref[b, e]
            device = block >> 1
            section = (device * 1366) >> 16
            group = device - section * N_GRP
            at = (section & 1) * N_Y + (section >> 1)
            row = group * 4 + (at & 3)
            shift = (128 - (at >> 2) * 32 - (block & 1) * 16) & 127
            line = moments_ref[pl.ds(row, 1), :]
            picked_ref[b * FAR + e : b * FAR + e + 1, :] = pltpu.roll(line, shift, 1)
    out = []
    for b in range(2):
        picked = picked_ref[FAR * b : FAR * b + FAR, :]
        mass, cx, cy, cz, qxx, qyy, qzz, qxy, qxz, qyz = [picked[:, c : c + 1] for c in range(10)]
        x, y, z = [own_ref[c : c + 1, B * b : B * b + B] for c in range(3)]
        x, y, z = x - cx, y - cy, z - cz
        square = x * x + y * y + z * z + softening
        inverse = lax.rsqrt(square)
        two = inverse * inverse
        three = inverse * two
        five = three * two
        seven = five * two
        quad_x = qxx * x + qxy * y + qxz * z
        quad_y = qxy * x + qyy * y + qyz * z
        quad_z = qxz * x + qyz * y + qzz * z
        along = 2.5 * (x * quad_x + y * quad_y + z * quad_z) * seven - mass * three
        out.append(
            jnp.concatenate(
                [
                    jnp.sum(along * r - quad * five, axis=0, keepdims=True)
                    for r, quad in ((x, quad_x), (y, quad_y), (z, quad_z))
                ],
                0,
            )
        )
    return jnp.concatenate(out, 1)


def first_step(own_ref, vel_ref, direct_ref, moments_ref, far_ref, send_ref, next_ref, speed_ref, picked_ref):
    accel = direct_ref[...] + far_field(own_ref, moments_ref, far_ref, picked_ref)
    speed = vel_ref[...] + timestep * accel
    speed_ref[...] = speed
    current = own_ref[0:3, :] + (0.5 * timestep) * speed
    half = current + (0.5 * timestep) * speed
    own = jnp.concatenate([half, own_ref[3:4, :]], 0)
    next_ref[...] = own
    for d in range(N_Y):
        send_ref[d] = own


def last_step(own_ref, vel_ref, direct_ref, moments_ref, far_ref, pos_ref, speed_ref, accel_ref, picked_ref):
    accel = direct_ref[...] + far_field(own_ref, moments_ref, far_ref, picked_ref)
    accel_ref[...] = accel
    speed = vel_ref[...] + timestep * accel
    speed_ref[...] = speed
    pos_ref[...] = own_ref[0:3, :] + (0.5 * timestep) * speed


def on_device(positions, velocities, masses, near_list, near_count, far_list):
    send, own = pl.pallas_call(
        opening,
        out_shape=(shape(N_Y, 4, W), shape(4, W)),
        in_specs=[pl.BlockSpec(memory_space=pl.ANY)] * 3,
        out_specs=(VMEM, VMEM),
        scratch_shapes=[
            pltpu.VMEM((3, W), f32),
            pltpu.VMEM((3, W), f32),
            pltpu.VMEM((1, W), f32),
            pltpu.SemaphoreType.DMA((3,)),
        ],
        compiler_params=WHOLE,
    )(positions, velocities, masses.reshape(1, W))
    speed = velocities
    for step in range(2):
        along = lax.all_to_all(send, "y", split_axis=0, concat_axis=0, tiled=True)
        ghosts = lax.all_gather(along, "core", axis=0, tiled=True)
        message = pl.pallas_call(
            group_moments,
            out_shape=shape(N_GRP, 4, 128),
            in_specs=[VMEM],
            out_specs=VMEM,
            compiler_params=PARAMS,
        )(ghosts)
        moments = lax.all_to_all(message, "grp", split_axis=0, concat_axis=0, tiled=True)
        near = pl.pallas_call(
            direct,
            out_shape=shape(3, W),
            in_specs=[VMEM, VMEM, VMEM, SMEM],
            out_specs=VMEM,
            scratch_shapes=[
                pltpu.VMEM((48, N_SEC * W), bf16),
                pltpu.VMEM((32, N_SEC * W), bf16),
                pltpu.VMEM((32, W), f32),
                pltpu.VMEM((2, KBLK, 128), f32),
            ],
            compiler_params=PARAMS,
            cost_estimate=pl.CostEstimate(
                flops=2 * 80 * W * N_SEC * W, bytes_accessed=200000, transcendentals=W * N_SEC * W
            ),
        )(own, ghosts, near_list, near_count)
        last = step == 1
        made = pl.pallas_call(
            last_step if last else first_step,
            out_shape=(shape(3, W),) * 3 if last else (shape(N_Y, 4, W), shape(4, W), shape(3, W)),
            in_specs=[VMEM, VMEM, VMEM, VMEM, SMEM],
            out_specs=(VMEM,) * 3,
            scratch_shapes=[pltpu.VMEM((2 * FAR, 128), f32)],
            compiler_params=PARAMS,
        )(own, speed, near, moments.reshape(N_GRP * 4, 128), far_list)
        if last:
            return made
        send, own, speed = made


def solution(mesh):
    parts = jax.sharding.Mesh(mesh.devices.reshape(N_Y, 2, N_GRP), ("y", "core", "grp"))
    every = ("y", "core", "grp")
    placed = (P(None, every), P(None, every), P(every), P(every, None), P(every), P(every, None))
    return jax.shard_map(
        on_device,
        mesh=parts,
        in_specs=placed,
        out_specs=(P(None, every),) * 3,
        check_vma=False,
    )
```

```python
import jax
import jax.numpy as jnp
from jax import lax
from jax.experimental import pallas as pl
from jax.experimental.pallas import tpu as pltpu
from jax.sharding import PartitionSpec as P

timestep = 0.05
softening = 0.25
N_SEC = 16
N_GRP = 48
B = 256
W = 2 * B
KBLK = 2 * N_SEC
LIST = 64
FAR = 32
CHUNK = 1024
f32 = jnp.float32
bf16 = jnp.bfloat16
VMEM = pl.BlockSpec(memory_space=pltpu.VMEM)
SMEM = pl.BlockSpec(memory_space=pltpu.SMEM)
PARAMS = pltpu.CompilerParams(vmem_limit_bytes=40 * 1024 * 1024)


def shape(*dims):
    return jax.ShapeDtypeStruct(dims, f32)


def split3(value):
    first = value.astype(bf16).astype(f32)
    rest = value - first
    second = rest.astype(bf16).astype(f32)
    return first, second, rest - second


def opening(pos_hbm, vel_hbm, mass_hbm, send_ref, own_ref, pos_ref, vel_ref, mass_ref, sems):
    copies = [
        pltpu.make_async_copy(source, target, sems.at[i])
        for i, (source, target) in enumerate(((pos_hbm, pos_ref), (vel_hbm, vel_ref), (mass_hbm, mass_ref)))
    ]
    for copy in copies:
        copy.start()
    for copy in copies:
        copy.wait()
    half = pos_ref[...] + (0.5 * timestep) * vel_ref[...]
    own = jnp.concatenate([half, mass_ref[...]], 0)
    own_ref[...] = own
    for d in range(N_SEC):
        send_ref[d] = own


def group_moments(ghost_ref, out_ref):
    section = lax.broadcasted_iota(jnp.int32, (N_SEC, 128), 0)
    lane = lax.broadcasted_iota(jnp.int32, (N_SEC, 128), 1)
    base = section // 4 * 32
    packed = jnp.zeros((N_SEC, 128), f32)
    whole = [ghost_ref[:, c, :] for c in range(4)]

    def total(v):
        return jnp.sum(v, axis=1, keepdims=True)

    for place in range(2):
        x, y, z, m = [w[:, B * place : B * place + B] for w in whole]
        mass = total(m)
        centre = [total(m * v) / mass for v in (x, y, z)]
        dx, dy, dz = [v - c for v, c in zip((x, y, z), centre)]
        radius = dx * dx + dy * dy + dz * dz
        m3 = 3.0 * m
        numbers = [
            mass,
            *centre,
            total(m * (3.0 * dx * dx - radius)),
            total(m * (3.0 * dy * dy - radius)),
            total(m * (3.0 * dz * dz - radius)),
            total(m3 * dx * dy),
            total(m3 * dx * dz),
            total(m3 * dy * dz),
        ]
        for c, number in enumerate(numbers):
            packed = jnp.where(lane == base + (16 * place + c), number, packed)
    message = packed[0:4] + packed[4:8] + packed[8:12] + packed[12:16]
    for k in range(N_GRP):
        out_ref[k] = message


def direct(own_ref, ghost_ref, near_ref, count_ref, out_ref, source_ref, weight_ref, total_ref, times_ref):
    block = lax.broadcasted_iota(jnp.int32, (KBLK, LIST), 0)
    slot = lax.broadcasted_iota(jnp.int32, (KBLK, LIST), 1)
    for b in range(2):
        hit = (near_ref[b : b + 1, :] == block) & (slot < count_ref[b])
        times = jnp.sum(jnp.where(hit, 1.0, 0.0).astype(f32), axis=1, keepdims=True)
        times_ref[b] = jnp.broadcast_to(times, (KBLK, 128))
    tot = ghost_ref[0]
    for d in range(1, N_SEC):
        tot = tot + ghost_ref[d]
    middle = jnp.sum(tot, axis=1, keepdims=True)[0:3] * (1.0 / (N_SEC * W))
    target = own_ref[0:3, :] - middle
    norm = jnp.sum(target * target, axis=0, keepdims=True) + softening
    pad = jnp.zeros((3, W), f32)
    a, b, c = split3(jnp.concatenate([-2.0 * target, jnp.ones((1, W), f32), norm, pad], 0))
    targets = jnp.concatenate([a, a, a, b, b, c], 0).astype(bf16)
    for d in range(N_SEC):
        ghost = ghost_ref[d]
        source = ghost[0:3] - middle
        mass = ghost[3:4]
        square = jnp.sum(source * source, axis=0, keepdims=True)
        a, b, c = split3(jnp.concatenate([source, square, jnp.ones((1, W), f32), pad], 0))
        source_ref[:, W * d : W * d + W] = jnp.concatenate([a, b, c, a, b, a], 0).astype(bf16)
        terms = jnp.concatenate([mass, source * mass], 0)
        k = 2 * d
        both = []
        for t in range(2):
            first, second = times_ref[t, k : k + 1, :], times_ref[t, k + 1 : k + 2, :]
            both.append(terms * jnp.concatenate([first, first, second, second], 1))
        a, b, c = split3(jnp.concatenate(both, 0))
        weight_ref[:, W * d : W * d + W] = jnp.concatenate([a, b, c, jnp.zeros_like(a)], 0).astype(bf16)
    total_ref[...] = jnp.zeros_like(total_ref)

    @pl.loop(0, N_SEC * W // CHUNK, unroll=2)
    def _(step):
        at = pl.ds(pl.multiple_of(step * CHUNK, CHUNK), CHUNK)
        square = lax.dot_general(
            source_ref[:, at], targets, (((0,), (0,)), ((), ())), preferred_element_type=f32
        )
        inverse = lax.rsqrt(square)
        cube = inverse * inverse * inverse
        high = cube.astype(bf16)
        low = (cube - high.astype(f32)).astype(bf16)
        weight = weight_ref[:, at]
        total_ref[...] += jnp.dot(weight, high, preferred_element_type=f32) + jnp.dot(
            weight, low, preferred_element_type=f32
        )

    sums = total_ref[0:8] + total_ref[8:16] + total_ref[16:24]
    lane = lax.broadcasted_iota(jnp.int32, (4, W), 1)
    sums = jnp.where(lane < B, sums[0:4], sums[4:8])
    out_ref[...] = sums[1:4] - target * sums[0:1]


def far_field(own_ref, moments_ref, far_ref, picked_ref):
    for b in range(2):
        for e in range(FAR):
            block = far_ref[b, e]
            device = block >> 1
            section = (device * 1366) >> 16
            group = device - section * N_GRP
            row = group * 4 + (section & 3)
            shift = (128 - (section >> 2) * 32 - (block & 1) * 16) & 127
            line = moments_ref[pl.ds(row, 1), :]
            picked_ref[b * FAR + e : b * FAR + e + 1, :] = pltpu.roll(line, shift, 1)
    out = []
    for b in range(2):
        picked = picked_ref[FAR * b : FAR * b + FAR, :]
        mass, cx, cy, cz, qxx, qyy, qzz, qxy, qxz, qyz = [picked[:, c : c + 1] for c in range(10)]
        x, y, z = [own_ref[c : c + 1, B * b : B * b + B] for c in range(3)]
        x, y, z = x - cx, y - cy, z - cz
        square = x * x + y * y + z * z + softening
        inverse = lax.rsqrt(square)
        two = inverse * inverse
        three = inverse * two
        five = three * two
        seven = five * two
        quad_x = qxx * x + qxy * y + qxz * z
        quad_y = qxy * x + qyy * y + qyz * z
        quad_z = qxz * x + qyz * y + qzz * z
        along = 2.5 * (x * quad_x + y * quad_y + z * quad_z) * seven - mass * three
        out.append(
            jnp.concatenate(
                [
                    jnp.sum(along * r - quad * five, axis=0, keepdims=True)
                    for r, quad in ((x, quad_x), (y, quad_y), (z, quad_z))
                ],
                0,
            )
        )
    return jnp.concatenate(out, 1)


def first_step(own_ref, vel_ref, direct_ref, moments_ref, far_ref, send_ref, next_ref, speed_ref, picked_ref):
    accel = direct_ref[...] + far_field(own_ref, moments_ref, far_ref, picked_ref)
    speed = vel_ref[...] + timestep * accel
    speed_ref[...] = speed
    current = own_ref[0:3, :] + (0.5 * timestep) * speed
    half = current + (0.5 * timestep) * speed
    own = jnp.concatenate([half, own_ref[3:4, :]], 0)
    next_ref[...] = own
    for d in range(N_SEC):
        send_ref[d] = own


def last_step(own_ref, vel_ref, direct_ref, moments_ref, far_ref, pos_ref, speed_ref, accel_ref, picked_ref):
    accel = direct_ref[...] + far_field(own_ref, moments_ref, far_ref, picked_ref)
    accel_ref[...] = accel
    speed = vel_ref[...] + timestep * accel
    speed_ref[...] = speed
    pos_ref[...] = own_ref[0:3, :] + (0.5 * timestep) * speed


def on_device(positions, velocities, masses, near_list, near_count, far_list):
    send, own = pl.pallas_call(
        opening,
        out_shape=(shape(N_SEC, 4, W), shape(4, W)),
        in_specs=[pl.BlockSpec(memory_space=pl.ANY)] * 3,
        out_specs=(VMEM, VMEM),
        scratch_shapes=[
            pltpu.VMEM((3, W), f32),
            pltpu.VMEM((3, W), f32),
            pltpu.VMEM((1, W), f32),
            pltpu.SemaphoreType.DMA((3,)),
        ],
        compiler_params=PARAMS,
    )(*[pltpu.with_memory_space_constraint(v, pltpu.HBM) for v in (positions, velocities, masses.reshape(1, W))])
    speed = velocities
    for step in range(2):
        ghosts = lax.all_to_all(send, "sec", split_axis=0, concat_axis=0, tiled=True)
        message = pl.pallas_call(
            group_moments,
            out_shape=shape(N_GRP, 4, 128),
            in_specs=[VMEM],
            out_specs=VMEM,
            compiler_params=PARAMS,
        )(ghosts)
        moments = lax.all_to_all(message, "grp", split_axis=0, concat_axis=0, tiled=True)
        near = pl.pallas_call(
            direct,
            out_shape=shape(3, W),
            in_specs=[VMEM, VMEM, VMEM, SMEM],
            out_specs=VMEM,
            scratch_shapes=[
                pltpu.VMEM((48, N_SEC * W), bf16),
                pltpu.VMEM((32, N_SEC * W), bf16),
                pltpu.VMEM((32, W), f32),
                pltpu.VMEM((2, KBLK, 128), f32),
            ],
            compiler_params=PARAMS,
            cost_estimate=pl.CostEstimate(
                flops=2 * 80 * W * N_SEC * W, bytes_accessed=200000, transcendentals=W * N_SEC * W
            ),
        )(own, ghosts, near_list, near_count)
        last = step == 1
        made = pl.pallas_call(
            last_step if last else first_step,
            out_shape=(shape(3, W),) * 3 if last else (shape(N_SEC, 4, W), shape(4, W), shape(3, W)),
            in_specs=[VMEM, VMEM, VMEM, VMEM, SMEM],
            out_specs=(VMEM,) * 3,
            scratch_shapes=[pltpu.VMEM((2 * FAR, 128), f32)],
            compiler_params=PARAMS,
        )(own, speed, near, moments.reshape(N_GRP * 4, 128), far_list)
        if last:
            return made
        send, own, speed = made


def solution(mesh):
    every = ("sec", "grp")
    placed = (P(None, every), P(None, every), P(every), P(every, None), P(every), P(every, None))
    return jax.shard_map(
        on_device,
        mesh=mesh,
        in_specs=placed,
        out_specs=(P(None, every),) * 3,
        check_vma=False,
    )
```

```python
import jax
import jax.numpy as jnp
from jax import lax
from jax.experimental import pallas as pl
from jax.experimental.pallas import tpu as pltpu
from jax.sharding import PartitionSpec as P

timestep = 0.05
softening = 0.25
N_SEC = 16
N_GRP = 48
B = 256
W = 2 * B
KBLK = 2 * N_SEC
LIST = 64
FAR = 32
CHUNK = 1024
LINE = 4 * W + 128
f32 = jnp.float32
bf16 = jnp.bfloat16
VMEM = pl.BlockSpec(memory_space=pltpu.VMEM)
SMEM = pl.BlockSpec(memory_space=pltpu.SMEM)
PARAMS = pltpu.CompilerParams(vmem_limit_bytes=40 * 1024 * 1024)


def shape(*dims):
    return jax.ShapeDtypeStruct(dims, f32)


def split3(value):
    first = value.astype(bf16).astype(f32)
    rest = value - first
    second = rest.astype(bf16).astype(f32)
    return first, second, rest - second


def opening(pos_hbm, vel_hbm, mass_hbm, far_ref, send_ref, own_ref, pos_ref, vel_ref, mass_ref, lists_ref, sems):
    copies = [
        pltpu.make_async_copy(source, target, sems.at[i])
        for i, (source, target) in enumerate(((pos_hbm, pos_ref), (vel_hbm, vel_ref), (mass_hbm, mass_ref)))
    ]
    for copy in copies:
        copy.start()
    lists_ref[...] = jnp.zeros_like(lists_ref)
    lists_ref[0:2, 0:FAR] = far_ref[...].astype(f32)
    lists = lists_ref[0:1, :] + pltpu.roll(lists_ref[1:2, :], FAR, 1)
    for copy in copies:
        copy.wait()
    half = pos_ref[...] + (0.5 * timestep) * vel_ref[...]
    own_ref[...] = jnp.concatenate([half, mass_ref[...]], 0)
    line = jnp.concatenate([half[0:1], half[1:2], half[2:3], mass_ref[...], lists], 1)
    for d in range(N_SEC):
        send_ref[d] = line


def moments_message(whole):
    section = lax.broadcasted_iota(jnp.int32, (N_SEC, 128), 0)
    lane = lax.broadcasted_iota(jnp.int32, (N_SEC, 128), 1)
    base = section // 4 * 32
    packed = jnp.zeros((N_SEC, 128), f32)

    def total(v):
        return jnp.sum(v, axis=1, keepdims=True)

    for place in range(2):
        x, y, z, m = [w[:, B * place : B * place + B] for w in whole]
        mass = total(m)
        centre = [total(m * v) / mass for v in (x, y, z)]
        dx, dy, dz = [v - c for v, c in zip((x, y, z), centre)]
        radius = dx * dx + dy * dy + dz * dz
        m3 = 3.0 * m
        numbers = [
            mass,
            *centre,
            total(m * (3.0 * dx * dx - radius)),
            total(m * (3.0 * dy * dy - radius)),
            total(m * (3.0 * dz * dz - radius)),
            total(m3 * dx * dy),
            total(m3 * dx * dz),
            total(m3 * dy * dz),
        ]
        for c, number in enumerate(numbers):
            packed = jnp.where(lane == base + (16 * place + c), number, packed)
    return packed[0:4] + packed[4:8] + packed[8:12] + packed[12:16]


def group_moments(ghost_ref, out_ref):
    message = moments_message([ghost_ref[:, 0, W * c : W * c + W] for c in range(4)])
    for k in range(N_GRP):
        out_ref[k] = message


def direct(own_ref, near_ref, count_ref, fetch, source_ref, weight_ref, total_ref, times_ref):
    block = lax.broadcasted_iota(jnp.int32, (KBLK, LIST), 0)
    slot = lax.broadcasted_iota(jnp.int32, (KBLK, LIST), 1)
    for b in range(2):
        hit = (near_ref[b : b + 1, :] == block) & (slot < count_ref[b])
        times = jnp.sum(jnp.where(hit, 1.0, 0.0).astype(f32), axis=1, keepdims=True)
        times_ref[b] = jnp.broadcast_to(times, (KBLK, 128))
    middle = jnp.sum(own_ref[0:3, :], axis=1, keepdims=True) * (1.0 / W)
    target = own_ref[0:3, :] - middle
    norm = jnp.sum(target * target, axis=0, keepdims=True) + softening
    pad = jnp.zeros((3, W), f32)
    a, b, c = split3(jnp.concatenate([-2.0 * target, jnp.ones((1, W), f32), norm, pad], 0))
    targets = jnp.concatenate([a, a, a, b, b, c], 0).astype(bf16)
    for d in range(N_SEC):
        ghost = fetch(d)
        source = ghost[0:3] - middle
        mass = ghost[3:4]
        square = jnp.sum(source * source, axis=0, keepdims=True)
        a, b, c = split3(jnp.concatenate([source, square, jnp.ones((1, W), f32), pad], 0))
        source_ref[:, W * d : W * d + W] = jnp.concatenate([a, b, c, a, b, a], 0).astype(bf16)
        terms = jnp.concatenate([mass, source * mass], 0)
        k = 2 * d
        both = []
        for t in range(2):
            first, second = times_ref[t, k : k + 1, :], times_ref[t, k + 1 : k + 2, :]
            both.append(terms * jnp.concatenate([first, first, second, second], 1))
        a, b, c = split3(jnp.concatenate(both, 0))
        weight_ref[:, W * d : W * d + W] = jnp.concatenate([a, b, c, jnp.zeros_like(a)], 0).astype(bf16)
    total_ref[...] = jnp.zeros_like(total_ref)

    @pl.loop(0, N_SEC * W // CHUNK, unroll=2)
    def _(step):
        at = pl.ds(pl.multiple_of(step * CHUNK, CHUNK), CHUNK)
        square = lax.dot_general(
            source_ref[:, at], targets, (((0,), (0,)), ((), ())), preferred_element_type=f32
        )
        inverse = lax.rsqrt(square)
        cube = inverse * inverse * inverse
        high = cube.astype(bf16)
        low = (cube - high.astype(f32)).astype(bf16)
        weight = weight_ref[:, at]
        total_ref[...] += jnp.dot(weight, high, preferred_element_type=f32) + jnp.dot(
            weight, low, preferred_element_type=f32
        )

    sums = total_ref[0:8] + total_ref[8:16] + total_ref[16:24]
    lane = lax.broadcasted_iota(jnp.int32, (4, W), 1)
    sums = jnp.where(lane < B, sums[0:4], sums[4:8])
    return sums[1:4] - target * sums[0:1]


def first_direct(own_ref, ghost_ref, near_ref, count_ref, vel_ref, out_ref, send_ref, *scratch):
    def fetch(d):
        return jnp.concatenate([ghost_ref[d, :, W * c : W * c + W] for c in range(4)], 0)

    near = direct(own_ref, near_ref, count_ref, fetch, *scratch)
    out_ref[...] = near
    start = own_ref[0:3, :] + timestep * (vel_ref[...] + timestep * near)
    line = jnp.concatenate([start[0:1], start[1:2], start[2:3]], 1)
    for d in range(N_SEC):
        send_ref[d] = line


def last_direct(own_ref, ghost_ref, half_ref, near_ref, count_ref, out_ref, *scratch):
    def fetch(d):
        rows = [half_ref[c, d : d + 1, :] for c in range(3)]
        return jnp.concatenate([*rows, ghost_ref[d, :, 3 * W : 4 * W]], 0)

    out_ref[...] = direct(own_ref, near_ref, count_ref, fetch, *scratch)


def place_of(block):
    device = block >> 1
    section = (device * 1366) >> 16
    group = device - section * N_GRP
    return group * 4 + (section & 3), (section >> 2) * 2 + (block & 1)


def far_sum(x, y, z, picked):
    mass, cx, cy, cz, qxx, qyy, qzz, qxy, qxz, qyz = [picked[:, c : c + 1] for c in range(10)]
    x, y, z = x - cx, y - cy, z - cz
    square = x * x + y * y + z * z + softening
    inverse = lax.rsqrt(square)
    two = inverse * inverse
    five = two * two * inverse
    quad_x = qxx * x + qxy * y + qxz * z
    quad_y = qxy * x + qyy * y + qyz * z
    quad_z = qxz * x + qyz * y + qzz * z
    along = 2.5 * (x * quad_x + y * quad_y + z * quad_z) * two - mass * square
    return [
        jnp.sum((along * r - quad) * five, axis=0, keepdims=True)
        for r, quad in ((x, quad_x), (y, quad_y), (z, quad_z))
    ]


def group_far(ghost_ref, moments_ref, out_ref, hot_ref):
    entries = ghost_ref[:, 0, 4 * W : LINE].astype(jnp.int32)
    row, which = place_of(entries)
    rows = N_GRP * 4
    number = lax.broadcasted_iota(jnp.int32, (rows, 128), 0)
    for d in range(N_SEC):
        hot_ref[:, 128 * d : 128 * d + 128] = jnp.where(number == row[d : d + 1, :], 1.0, 0.0).astype(bf16)
    hot = hot_ref[...]
    picked = sum(
        lax.dot_general(part.astype(bf16), hot, (((0,), (0,)), ((), ())), preferred_element_type=f32)
        for part in split3(moments_ref[...])
    )
    for d in range(N_SEC):
        lines = picked[:, 128 * d : 128 * d + 128]
        mine = lines[0:16]
        for k in range(1, 8):
            mine = jnp.where(which[d : d + 1, :] == k, lines[16 * k : 16 * k + 16], mine)
        mine = mine.T
        for place in range(2):
            at = B * place
            x, y, z = [ghost_ref[d, :, W * c + at : W * c + at + B] for c in range(3)]
            parts = far_sum(x, y, z, mine[FAR * place : FAR * place + FAR])
            for c in range(3):
                out_ref[c, d : d + 1, at : at + B] = parts[c]


def second_moments(start_ref, far_ref, ghost_ref, vel_ref, near_ref, own_ref, out_ref, half_ref, next_ref, speed_ref):
    whole = []
    for c in range(3):
        half = start_ref[:, 0, W * c : W * c + W] + (timestep * timestep) * far_ref[c]
        half_ref[c] = half
        whole.append(half)
    message = moments_message([*whole, ghost_ref[:, 0, 3 * W : 4 * W]])
    for k in range(N_GRP):
        out_ref[k] = message
    section = lax.axis_index("sec")
    far = jnp.concatenate([far_ref[c, pl.ds(section, 1), :] for c in range(3)], 0)
    speed = vel_ref[...] + timestep * (near_ref[...] + far)
    speed_ref[...] = speed
    next_ref[...] = jnp.concatenate([own_ref[0:3, :] + timestep * speed, own_ref[3:4, :]], 0)


def last_step(own_ref, vel_ref, direct_ref, moments_ref, far_ref, pos_ref, speed_ref, accel_ref, picked_ref):
    for b in range(2):
        for e in range(FAR):
            row, which = place_of(far_ref[b, e])
            line = moments_ref[pl.ds(row, 1), :]
            picked_ref[b * FAR + e : b * FAR + e + 1, :] = pltpu.roll(line, (128 - which * 16) & 127, 1)
    far = []
    for b in range(2):
        x, y, z = [own_ref[c : c + 1, B * b : B * b + B] for c in range(3)]
        far.append(jnp.concatenate(far_sum(x, y, z, picked_ref[FAR * b : FAR * b + FAR, :]), 0))
    accel = direct_ref[...] + jnp.concatenate(far, 1)
    accel_ref[...] = accel
    speed = vel_ref[...] + timestep * accel
    speed_ref[...] = speed
    pos_ref[...] = own_ref[0:3, :] + (0.5 * timestep) * speed


def exchange(value, axis):
    return lax.all_to_all(value, axis, split_axis=0, concat_axis=0, tiled=True)


def on_device(positions, velocities, masses, near_list, near_count, far_list):
    message = shape(N_GRP, 4, 128)
    direct_scratch = [
        pltpu.VMEM((48, N_SEC * W), bf16),
        pltpu.VMEM((32, N_SEC * W), bf16),
        pltpu.VMEM((32, W), f32),
        pltpu.VMEM((2, KBLK, 128), f32),
    ]
    pairs = W * N_SEC * W
    direct_cost = pl.CostEstimate(flops=160 * pairs, bytes_accessed=200000, transcendentals=pairs)
    inputs = [pltpu.with_memory_space_constraint(v, pltpu.HBM) for v in (positions, velocities, masses.reshape(1, W))]
    send, own = pl.pallas_call(
        opening,
        out_shape=(shape(N_SEC, 1, LINE), shape(4, W)),
        in_specs=[pl.BlockSpec(memory_space=pl.ANY)] * 3 + [VMEM],
        out_specs=(VMEM, VMEM),
        scratch_shapes=[
            pltpu.VMEM((3, W), f32),
            pltpu.VMEM((3, W), f32),
            pltpu.VMEM((1, W), f32),
            pltpu.VMEM((8, 128), f32),
            pltpu.SemaphoreType.DMA((3,)),
        ],
        compiler_params=PARAMS,
    )(*inputs, far_list)
    ghosts = exchange(send, "sec")
    first = pl.pallas_call(
        group_moments,
        out_shape=message,
        in_specs=[VMEM],
        out_specs=VMEM,
        compiler_params=PARAMS,
    )(ghosts)
    moments = exchange(first, "grp").reshape(N_GRP * 4, 128)
    near, send = pl.pallas_call(
        first_direct,
        out_shape=(shape(3, W), shape(N_SEC, 1, 3 * W)),
        in_specs=[VMEM, VMEM, VMEM, SMEM, VMEM],
        out_specs=(VMEM, VMEM),
        scratch_shapes=direct_scratch,
        compiler_params=PARAMS,
        cost_estimate=direct_cost,
    )(own, ghosts, near_list, near_count, velocities)
    starts = exchange(send, "sec")
    far = pl.pallas_call(
        group_far,
        out_shape=shape(3, N_SEC, W),
        in_specs=[VMEM, VMEM],
        out_specs=VMEM,
        scratch_shapes=[pltpu.VMEM((N_GRP * 4, N_SEC * 128), bf16)],
        compiler_params=PARAMS,
        cost_estimate=pl.CostEstimate(flops=10**10, bytes_accessed=200000, transcendentals=10**6),
    )(ghosts, moments)
    second, halves, own, speed = pl.pallas_call(
        second_moments,
        out_shape=(message, shape(3, N_SEC, W), shape(4, W), shape(3, W)),
        in_specs=[VMEM] * 6,
        out_specs=(VMEM,) * 4,
        compiler_params=PARAMS,
    )(starts, far, ghosts, velocities, near, own)
    moments = exchange(second, "grp").reshape(N_GRP * 4, 128)
    near = pl.pallas_call(
        last_direct,
        out_shape=shape(3, W),
        in_specs=[VMEM, VMEM, VMEM, VMEM, SMEM],
        out_specs=VMEM,
        scratch_shapes=direct_scratch,
        compiler_params=PARAMS,
        cost_estimate=direct_cost,
    )(own, ghosts, halves, near_list, near_count)
    return pl.pallas_call(
        last_step,
        out_shape=(shape(3, W),) * 3,
        in_specs=[VMEM, VMEM, VMEM, VMEM, SMEM],
        out_specs=(VMEM,) * 3,
        scratch_shapes=[pltpu.VMEM((2 * FAR, 128), f32)],
        compiler_params=PARAMS,
    )(own, speed, near, moments, far_list)


def solution(mesh):
    every = ("sec", "grp")
    placed = (P(None, every), P(None, every), P(every), P(every, None), P(every), P(every, None))
    return jax.shard_map(
        on_device,
        mesh=mesh,
        in_specs=placed,
        out_specs=(P(None, every),) * 3,
        check_vma=False,
    )
```

```python
import jax
import jax.numpy as jnp
from jax import lax
from jax.experimental import pallas as pl
from jax.experimental.pallas import tpu as pltpu
from jax.sharding import PartitionSpec as P

timestep = 0.05
softening = 0.25
N_SEC = 16
N_GRP = 48
B = 256
W = 2 * B
KBLK = 2 * N_SEC
LIST = 64
FAR = 32
CHUNK = 1024
LINE = 4 * W + 128
f32 = jnp.float32
bf16 = jnp.bfloat16
VMEM = pl.BlockSpec(memory_space=pltpu.VMEM)
SMEM = pl.BlockSpec(memory_space=pltpu.SMEM)
PARAMS = pltpu.CompilerParams(vmem_limit_bytes=40 * 1024 * 1024)


def shape(*dims):
    return jax.ShapeDtypeStruct(dims, f32)


def split3(value):
    first = value.astype(bf16).astype(f32)
    rest = value - first
    second = rest.astype(bf16).astype(f32)
    return first, second, rest - second


def opening(
    pos_hbm, vel_hbm, mass_hbm, far_hbm, near_hbm, count_hbm, send_ref, own_ref, times_ref,
    pos_ref, vel_ref, mass_ref, far_ref, near_ref, count_ref, lists_ref, sems,
):
    pairs = (
        (pos_hbm, pos_ref),
        (vel_hbm, vel_ref),
        (mass_hbm, mass_ref),
        (far_hbm, far_ref),
        (near_hbm, near_ref),
        (count_hbm, count_ref),
    )
    copies = [pltpu.make_async_copy(source, target, sems.at[i]) for i, (source, target) in enumerate(pairs)]
    for copy in copies:
        copy.start()
    lists_ref[...] = jnp.zeros_like(lists_ref)
    for copy in copies:
        copy.wait()
    lists_ref[0:2, 0:FAR] = far_ref[...].astype(f32)
    lists = lists_ref[0:1, :] + pltpu.roll(lists_ref[1:2, :], FAR, 1)
    half = pos_ref[...] + (0.5 * timestep) * vel_ref[...]
    own_ref[...] = jnp.concatenate([half, mass_ref[...]], 0)
    line = jnp.concatenate([half[0:1], half[1:2], half[2:3], mass_ref[...], lists], 1)
    for d in range(N_SEC):
        send_ref[d] = line
    block = lax.broadcasted_iota(jnp.int32, (KBLK, LIST), 0)
    slot = lax.broadcasted_iota(jnp.int32, (KBLK, LIST), 1)
    for b in range(2):
        hit = (near_ref[b : b + 1, :] == block) & (slot < count_ref[b])
        times = jnp.sum(jnp.where(hit, 1.0, 0.0).astype(f32), axis=1, keepdims=True)
        times_ref[b] = jnp.broadcast_to(times, (KBLK, 128))


def moments_message(whole):
    section = lax.broadcasted_iota(jnp.int32, (N_SEC, 128), 0)
    lane = lax.broadcasted_iota(jnp.int32, (N_SEC, 128), 1)
    base = section // 4 * 32
    packed = jnp.zeros((N_SEC, 128), f32)

    def total(v):
        return jnp.sum(v, axis=1, keepdims=True)

    for place in range(2):
        x, y, z, m = [w[:, B * place : B * place + B] for w in whole]
        mass = total(m)
        centre = [total(m * v) / mass for v in (x, y, z)]
        dx, dy, dz = [v - c for v, c in zip((x, y, z), centre)]
        radius = dx * dx + dy * dy + dz * dz
        m3 = 3.0 * m
        numbers = [
            mass,
            *centre,
            total(m * (3.0 * dx * dx - radius)),
            total(m * (3.0 * dy * dy - radius)),
            total(m * (3.0 * dz * dz - radius)),
            total(m3 * dx * dy),
            total(m3 * dx * dz),
            total(m3 * dy * dz),
        ]
        for c, number in enumerate(numbers):
            packed = jnp.where(lane == base + (16 * place + c), number, packed)
    return packed[0:4] + packed[4:8] + packed[8:12] + packed[12:16]


def group_moments(ghost_ref, out_ref):
    message = moments_message([ghost_ref[:, 0, W * c : W * c + W] for c in range(4)])
    for k in range(N_GRP):
        out_ref[k] = message


def direct(own_ref, times_ref, fetch, source_ref, weight_ref):
    middle = jnp.sum(own_ref[0:3, :], axis=1, keepdims=True) * (1.0 / W)
    target = own_ref[0:3, :] - middle
    norm = jnp.sum(target * target, axis=0, keepdims=True) + softening
    pad = jnp.zeros((3, W), f32)
    a, b, c = split3(jnp.concatenate([-2.0 * target, jnp.ones((1, W), f32), norm, pad], 0))
    targets = jnp.concatenate([a, a, a, b, b, c], 0).astype(bf16)
    for d in range(N_SEC):
        ghost = fetch(d)
        source = ghost[0:3] - middle
        mass = ghost[3:4]
        square = jnp.sum(source * source, axis=0, keepdims=True)
        a, b, c = split3(jnp.concatenate([source, square, jnp.ones((1, W), f32), pad], 0))
        source_ref[:, W * d : W * d + W] = jnp.concatenate([a, b, c, a, b, a], 0).astype(bf16)
        terms = jnp.concatenate([mass, source * mass], 0)
        k = 2 * d
        both = []
        for t in range(2):
            first, second = times_ref[t, k : k + 1, :], times_ref[t, k + 1 : k + 2, :]
            both.append(terms * jnp.concatenate([first, first, second, second], 1))
        a, b, c = split3(jnp.concatenate(both, 0))
        weight_ref[:, W * d : W * d + W] = jnp.concatenate([a, b, c, jnp.zeros_like(a)], 0).astype(bf16)
    total = jnp.zeros((32, W), f32)
    for start in range(0, N_SEC * W, CHUNK):
        square = lax.dot_general(
            source_ref[:, start : start + CHUNK],
            targets,
            (((0,), (0,)), ((), ())),
            preferred_element_type=f32,
        )
        inverse = lax.rsqrt(square)
        cube = inverse * inverse * inverse
        high = cube.astype(bf16)
        low = (cube - high.astype(f32)).astype(bf16)
        weight = weight_ref[:, start : start + CHUNK]
        total = total + jnp.dot(
            jnp.concatenate([weight, weight], 1), jnp.concatenate([high, low], 0), preferred_element_type=f32
        )
    sums = total[0:8] + total[8:16] + total[16:24]
    lane = lax.broadcasted_iota(jnp.int32, (4, W), 1)
    sums = jnp.where(lane < B, sums[0:4], sums[4:8])
    return sums[1:4] - target * sums[0:1]


def first_direct(own_ref, ghost_ref, times_ref, vel_ref, out_ref, send_ref, *scratch):
    def fetch(d):
        return jnp.concatenate([ghost_ref[d, :, W * c : W * c + W] for c in range(4)], 0)

    near = direct(own_ref, times_ref, fetch, *scratch)
    out_ref[...] = near
    start = own_ref[0:3, :] + timestep * (vel_ref[...] + timestep * near)
    line = jnp.concatenate([start[0:1], start[1:2], start[2:3]], 1)
    for d in range(N_SEC):
        send_ref[d] = line


def last_direct(own_ref, ghost_ref, half_ref, times_ref, out_ref, *scratch):
    def fetch(d):
        rows = [half_ref[c, d : d + 1, :] for c in range(3)]
        return jnp.concatenate([*rows, ghost_ref[d, :, 3 * W : 4 * W]], 0)

    out_ref[...] = direct(own_ref, times_ref, fetch, *scratch)


def place_of(block):
    device = block >> 1
    section = (device * 1366) >> 16
    group = device - section * N_GRP
    return group * 4 + (section & 3), (section >> 2) * 2 + (block & 1)


def far_sum(x, y, z, picked):
    mass, cx, cy, cz, qxx, qyy, qzz, qxy, qxz, qyz = [picked[:, c : c + 1] for c in range(10)]
    x, y, z = x - cx, y - cy, z - cz
    square = x * x + y * y + z * z + softening
    inverse = lax.rsqrt(square)
    two = inverse * inverse
    five = two * two * inverse
    quad_x = qxx * x + qxy * y + qxz * z
    quad_y = qxy * x + qyy * y + qyz * z
    quad_z = qxz * x + qyz * y + qzz * z
    along = 2.5 * (x * quad_x + y * quad_y + z * quad_z) * two - mass * square
    return [
        jnp.sum((along * r - quad) * five, axis=0, keepdims=True)
        for r, quad in ((x, quad_x), (y, quad_y), (z, quad_z))
    ]


def group_far(ghost_ref, moments_ref, far_ref, out_ref, hot_ref):
    entries = ghost_ref[:, 0, 4 * W : LINE].astype(jnp.int32)
    row, which = place_of(entries)
    rows = N_GRP * 4
    number = lax.broadcasted_iota(jnp.int32, (rows, 128), 0)
    for d in range(N_SEC):
        hot_ref[:, 128 * d : 128 * d + 128] = jnp.where(number == row[d : d + 1, :], 1.0, 0.0).astype(bf16)
    hot = hot_ref[...]
    picked = sum(
        lax.dot_general(part.astype(bf16), hot, (((0,), (0,)), ((), ())), preferred_element_type=f32)
        for part in split3(moments_ref[...])
    )
    for d in range(N_SEC):
        lines = picked[:, 128 * d : 128 * d + 128]
        mine = lines[0:16]
        for k in range(1, 8):
            mine = jnp.where(which[d : d + 1, :] == k, lines[16 * k : 16 * k + 16], mine)
        mine = mine.T
        for place in range(2):
            at = B * place
            x, y, z = [ghost_ref[d, :, W * c + at : W * c + at + B] for c in range(3)]
            parts = far_sum(x, y, z, mine[FAR * place : FAR * place + FAR])
            for c in range(3):
                out_ref[c, d : d + 1, at : at + B] = parts[c]


def second_moments(start_ref, far_ref, ghost_ref, vel_ref, near_ref, own_ref, out_ref, half_ref, next_ref, speed_ref):
    whole = []
    for c in range(3):
        half = start_ref[:, 0, W * c : W * c + W] + (timestep * timestep) * far_ref[c]
        half_ref[c] = half
        whole.append(half)
    message = moments_message([*whole, ghost_ref[:, 0, 3 * W : 4 * W]])
    for k in range(N_GRP):
        out_ref[k] = message
    section = lax.axis_index("sec")
    far = jnp.concatenate([far_ref[c, pl.ds(section, 1), :] for c in range(3)], 0)
    speed = vel_ref[...] + timestep * (near_ref[...] + far)
    speed_ref[...] = speed
    next_ref[...] = jnp.concatenate([own_ref[0:3, :] + timestep * speed, own_ref[3:4, :]], 0)


def last_step(own_ref, vel_ref, direct_ref, moments_ref, far_ref, pos_ref, speed_ref, accel_ref, picked_ref):
    for b in range(2):
        for e in range(FAR):
            row, which = place_of(far_ref[b, e])
            line = moments_ref[pl.ds(row, 1), :]
            picked_ref[b * FAR + e : b * FAR + e + 1, :] = pltpu.roll(line, (128 - which * 16) & 127, 1)
    far = []
    for b in range(2):
        x, y, z = [own_ref[c : c + 1, B * b : B * b + B] for c in range(3)]
        far.append(jnp.concatenate(far_sum(x, y, z, picked_ref[FAR * b : FAR * b + FAR, :]), 0))
    accel = direct_ref[...] + jnp.concatenate(far, 1)
    accel_ref[...] = accel
    speed = vel_ref[...] + timestep * accel
    speed_ref[...] = speed
    pos_ref[...] = own_ref[0:3, :] + (0.5 * timestep) * speed


def exchange(value, axis):
    return lax.all_to_all(value, axis, split_axis=0, concat_axis=0, tiled=True)


def on_device(positions, velocities, masses, near_list, near_count, far_list):
    message = shape(N_GRP, 4, 128)
    direct_scratch = [
        pltpu.VMEM((48, N_SEC * W), bf16),
        pltpu.VMEM((32, N_SEC * W), bf16),
    ]
    pairs = W * N_SEC * W
    direct_cost = pl.CostEstimate(flops=160 * pairs, bytes_accessed=200000, transcendentals=pairs)
    inputs = (positions, velocities, masses.reshape(1, W), far_list, near_list, near_count)
    send, own, times = pl.pallas_call(
        opening,
        out_shape=(shape(N_SEC, 1, LINE), shape(4, W), shape(2, KBLK, 128)),
        in_specs=[pl.BlockSpec(memory_space=pl.ANY)] * 6,
        out_specs=(VMEM,) * 3,
        scratch_shapes=[
            pltpu.VMEM((3, W), f32),
            pltpu.VMEM((3, W), f32),
            pltpu.VMEM((1, W), f32),
            pltpu.VMEM((2, FAR), jnp.int32),
            pltpu.VMEM((2, LIST), jnp.int32),
            pltpu.SMEM((2,), jnp.int32),
            pltpu.VMEM((8, 128), f32),
            pltpu.SemaphoreType.DMA((6,)),
        ],
        compiler_params=PARAMS,
    )(*[pltpu.with_memory_space_constraint(v, pltpu.HBM) for v in inputs])
    ghosts = exchange(send, "sec")
    first = pl.pallas_call(
        group_moments,
        out_shape=message,
        in_specs=[VMEM],
        out_specs=VMEM,
        compiler_params=PARAMS,
    )(ghosts)
    moments = exchange(first, "grp").reshape(N_GRP * 4, 128)
    near, send = pl.pallas_call(
        first_direct,
        out_shape=(shape(3, W), shape(N_SEC, 1, 3 * W)),
        in_specs=[VMEM] * 4,
        out_specs=(VMEM, VMEM),
        scratch_shapes=direct_scratch,
        compiler_params=PARAMS,
        cost_estimate=direct_cost,
    )(own, ghosts, times, velocities)
    starts = exchange(send, "sec")
    far = pl.pallas_call(
        group_far,
        out_shape=shape(3, N_SEC, W),
        in_specs=[VMEM, VMEM, SMEM],
        out_specs=VMEM,
        scratch_shapes=[pltpu.VMEM((N_GRP * 4, N_SEC * 128), bf16)],
        compiler_params=PARAMS,
        cost_estimate=pl.CostEstimate(flops=10**10, bytes_accessed=200000, transcendentals=10**6),
    )(ghosts, moments, far_list)
    second, halves, own, speed = pl.pallas_call(
        second_moments,
        out_shape=(message, shape(3, N_SEC, W), shape(4, W), shape(3, W)),
        in_specs=[VMEM] * 6,
        out_specs=(VMEM,) * 4,
        compiler_params=PARAMS,
    )(starts, far, ghosts, velocities, near, own)
    moments = exchange(second, "grp").reshape(N_GRP * 4, 128)
    near = pl.pallas_call(
        last_direct,
        out_shape=shape(3, W),
        in_specs=[VMEM] * 4,
        out_specs=VMEM,
        scratch_shapes=direct_scratch,
        compiler_params=PARAMS,
        cost_estimate=direct_cost,
    )(own, ghosts, halves, times)
    return pl.pallas_call(
        last_step,
        out_shape=(shape(3, W),) * 3,
        in_specs=[VMEM, VMEM, VMEM, VMEM, SMEM],
        out_specs=(VMEM,) * 3,
        scratch_shapes=[pltpu.VMEM((2 * FAR, 128), f32)],
        compiler_params=PARAMS,
    )(own, speed, near, moments, far_list)


def solution(mesh):
    every = ("sec", "grp")
    placed = (P(None, every), P(None, every), P(every), P(every, None), P(every), P(every, None))
    return jax.shard_map(
        on_device,
        mesh=mesh,
        in_specs=placed,
        out_specs=(P(None, every),) * 3,
        check_vma=False,
    )
```

```python
import jax
import jax.numpy as jnp
from jax import lax
from jax.experimental import pallas as pl
from jax.experimental.pallas import tpu as pltpu
from jax.sharding import PartitionSpec as P

timestep = 0.05
softening = 0.25
N_SEC = 16
N_GRP = 48
B = 256
W = 2 * B
KBLK = 2 * N_SEC
LIST = 64
FAR = 32
CHUNK = 1024
LINE = 4 * W + 128
f32 = jnp.float32
bf16 = jnp.bfloat16
VMEM = pl.BlockSpec(memory_space=pltpu.VMEM)
SMEM = pl.BlockSpec(memory_space=pltpu.SMEM)
PARAMS = pltpu.CompilerParams(vmem_limit_bytes=40 * 1024 * 1024)


def shape(*dims):
    return jax.ShapeDtypeStruct(dims, f32)


def split3(value):
    first = value.astype(bf16).astype(f32)
    rest = value - first
    second = rest.astype(bf16).astype(f32)
    return first, second, rest - second


def opening(
    pos_hbm, vel_hbm, mass_hbm, far_hbm, near_hbm, count_hbm, send_ref, own_ref, times_ref, spots_ref,
    pos_ref, vel_ref, mass_ref, far_ref, near_ref, count_ref, lists_ref, sems,
):
    pairs = (
        (pos_hbm, pos_ref),
        (vel_hbm, vel_ref),
        (mass_hbm, mass_ref),
        (far_hbm, far_ref),
        (near_hbm, near_ref),
        (count_hbm, count_ref),
    )
    copies = [pltpu.make_async_copy(source, target, sems.at[i]) for i, (source, target) in enumerate(pairs)]
    for copy in copies:
        copy.start()
    lists_ref[...] = jnp.zeros_like(lists_ref)
    for copy in copies:
        copy.wait()
    lists_ref[0:2, 0:FAR] = far_ref[...].astype(f32)
    lists = lists_ref[0:1, :] + pltpu.roll(lists_ref[1:2, :], FAR, 1)
    half = pos_ref[...] + (0.5 * timestep) * vel_ref[...]
    own_ref[...] = jnp.concatenate([half, mass_ref[...]], 0)
    line = jnp.concatenate([half[0:1], half[1:2], half[2:3], mass_ref[...], lists], 1)
    for d in range(N_SEC):
        send_ref[d] = line
    row, which = place_of(far_ref[...])
    spots_ref[0:2, :] = row
    spots_ref[2:4, :] = (128 - which * 16) & 127
    block = lax.broadcasted_iota(jnp.int32, (KBLK, LIST), 0)
    slot = lax.broadcasted_iota(jnp.int32, (KBLK, LIST), 1)
    for b in range(2):
        hit = (near_ref[b : b + 1, :] == block) & (slot < count_ref[b])
        times = jnp.sum(jnp.where(hit, 1.0, 0.0).astype(f32), axis=1, keepdims=True)
        times_ref[b] = jnp.broadcast_to(times, (KBLK, 128))


def moments_message(whole):
    section = lax.broadcasted_iota(jnp.int32, (N_SEC, 128), 0)
    lane = lax.broadcasted_iota(jnp.int32, (N_SEC, 128), 1)
    base = section // 4 * 32
    packed = jnp.zeros((N_SEC, 128), f32)

    def total(v):
        return jnp.sum(v, axis=1, keepdims=True)

    for place in range(2):
        x, y, z, m = [w[:, B * place : B * place + B] for w in whole]
        mass = total(m)
        centre = [total(m * v) / mass for v in (x, y, z)]
        dx, dy, dz = [v - c for v, c in zip((x, y, z), centre)]
        radius = dx * dx + dy * dy + dz * dz
        m3 = 3.0 * m
        numbers = [
            mass,
            *centre,
            total(m * (3.0 * dx * dx - radius)),
            total(m * (3.0 * dy * dy - radius)),
            total(m * (3.0 * dz * dz - radius)),
            total(m3 * dx * dy),
            total(m3 * dx * dz),
            total(m3 * dy * dz),
        ]
        for c, number in enumerate(numbers):
            packed = jnp.where(lane == base + (16 * place + c), number, packed)
    return packed[0:4] + packed[4:8] + packed[8:12] + packed[12:16]


def group_moments(ghost_ref, out_ref):
    message = moments_message([ghost_ref[:, 0, W * c : W * c + W] for c in range(4)])
    for k in range(N_GRP):
        out_ref[k] = message


def direct(own_ref, times_ref, fetch, source_ref, weight_ref):
    middle = jnp.sum(own_ref[0:3, :], axis=1, keepdims=True) * (1.0 / W)
    target = own_ref[0:3, :] - middle
    norm = jnp.sum(target * target, axis=0, keepdims=True) + softening
    pad = jnp.zeros((3, W), f32)
    a, b, c = split3(jnp.concatenate([-2.0 * target, jnp.ones((1, W), f32), norm, pad], 0))
    targets = jnp.concatenate([a, a, a, b, b, c], 0).astype(bf16)
    for d in range(N_SEC):
        ghost = fetch(d)
        source = ghost[0:3] - middle
        mass = ghost[3:4]
        square = jnp.sum(source * source, axis=0, keepdims=True)
        a, b, c = split3(jnp.concatenate([source, square, jnp.ones((1, W), f32), pad], 0))
        source_ref[:, W * d : W * d + W] = jnp.concatenate([a, b, c, a, b, a], 0).astype(bf16)
        terms = jnp.concatenate([mass, source * mass], 0)
        k = 2 * d
        both = []
        for t in range(2):
            first, second = times_ref[t, k : k + 1, :], times_ref[t, k + 1 : k + 2, :]
            both.append(terms * jnp.concatenate([first, first, second, second], 1))
        a, b, c = split3(jnp.concatenate(both, 0))
        weight_ref[:, W * d : W * d + W] = jnp.concatenate([a, b, c, jnp.zeros_like(a)], 0).astype(bf16)
    total = jnp.zeros((32, W), f32)
    for start in range(0, N_SEC * W, CHUNK):
        square = lax.dot_general(
            source_ref[:, start : start + CHUNK],
            targets,
            (((0,), (0,)), ((), ())),
            preferred_element_type=f32,
        )
        inverse = lax.rsqrt(square)
        cube = inverse * inverse * inverse
        high = cube.astype(bf16)
        low = (cube - high.astype(f32)).astype(bf16)
        weight = weight_ref[:, start : start + CHUNK]
        total = total + jnp.dot(
            jnp.concatenate([weight, weight], 1), jnp.concatenate([high, low], 0), preferred_element_type=f32
        )
    sums = total[0:8] + total[8:16] + total[16:24]
    lane = lax.broadcasted_iota(jnp.int32, (4, W), 1)
    sums = jnp.where(lane < B, sums[0:4], sums[4:8])
    return sums[1:4] - target * sums[0:1]


def first_direct(own_ref, ghost_ref, times_ref, vel_ref, out_ref, send_ref, *scratch):
    def fetch(d):
        return jnp.concatenate([ghost_ref[d, :, W * c : W * c + W] for c in range(4)], 0)

    near = direct(own_ref, times_ref, fetch, *scratch)
    out_ref[...] = near
    start = own_ref[0:3, :] + timestep * (vel_ref[...] + timestep * near)
    line = jnp.concatenate([start[0:1], start[1:2], start[2:3]], 1)
    for d in range(N_SEC):
        send_ref[d] = line


def last_direct(own_ref, ghost_ref, half_ref, times_ref, out_ref, *scratch):
    def fetch(d):
        rows = [half_ref[c, d : d + 1, :] for c in range(3)]
        return jnp.concatenate([*rows, ghost_ref[d, :, 3 * W : 4 * W]], 0)

    out_ref[...] = direct(own_ref, times_ref, fetch, *scratch)


def place_of(block):
    device = block >> 1
    section = (device * 1366) >> 16
    group = device - section * N_GRP
    return group * 4 + (section & 3), (section >> 2) * 2 + (block & 1)


def far_sum(x, y, z, picked):
    mass, cx, cy, cz, qxx, qyy, qzz, qxy, qxz, qyz = [picked[:, c : c + 1] for c in range(10)]
    x, y, z = x - cx, y - cy, z - cz
    square = x * x + y * y + z * z + softening
    inverse = lax.rsqrt(square)
    two = inverse * inverse
    five = two * two * inverse
    quad_x = qxx * x + qxy * y + qxz * z
    quad_y = qxy * x + qyy * y + qyz * z
    quad_z = qxz * x + qyz * y + qzz * z
    along = 2.5 * (x * quad_x + y * quad_y + z * quad_z) * two - mass * square
    return [
        jnp.sum((along * r - quad) * five, axis=0, keepdims=True)
        for r, quad in ((x, quad_x), (y, quad_y), (z, quad_z))
    ]


def group_far(ghost_ref, moments_ref, out_ref, hot_ref):
    entries = ghost_ref[:, 0, 4 * W : LINE].astype(jnp.int32)
    row, which = place_of(entries)
    rows = N_GRP * 4
    number = lax.broadcasted_iota(jnp.int32, (rows, 128), 0)
    for d in range(N_SEC):
        hot_ref[:, 128 * d : 128 * d + 128] = jnp.where(number == row[d : d + 1, :], 1.0, 0.0).astype(bf16)
    hot = hot_ref[...]
    picked = sum(
        lax.dot_general(part.astype(bf16), hot, (((0,), (0,)), ((), ())), preferred_element_type=f32)
        for part in split3(moments_ref[...])
    )
    for d in range(N_SEC):
        lines = picked[:, 128 * d : 128 * d + 128]
        mine = lines[0:16]
        for k in range(1, 8):
            mine = jnp.where(which[d : d + 1, :] == k, lines[16 * k : 16 * k + 16], mine)
        mine = mine.T
        for place in range(2):
            at = B * place
            x, y, z = [ghost_ref[d, :, W * c + at : W * c + at + B] for c in range(3)]
            parts = far_sum(x, y, z, mine[FAR * place : FAR * place + FAR])
            for c in range(3):
                out_ref[c, d : d + 1, at : at + B] = parts[c]


def second_moments(start_ref, far_ref, ghost_ref, vel_ref, near_ref, own_ref, out_ref, half_ref, next_ref, speed_ref):
    whole = []
    for c in range(3):
        half = start_ref[:, 0, W * c : W * c + W] + (timestep * timestep) * far_ref[c]
        half_ref[c] = half
        whole.append(half)
    message = moments_message([*whole, ghost_ref[:, 0, 3 * W : 4 * W]])
    for k in range(N_GRP):
        out_ref[k] = message
    section = lax.axis_index("sec")
    far = jnp.concatenate([far_ref[c, pl.ds(section, 1), :] for c in range(3)], 0)
    speed = vel_ref[...] + timestep * (near_ref[...] + far)
    speed_ref[...] = speed
    next_ref[...] = jnp.concatenate([own_ref[0:3, :] + timestep * speed, own_ref[3:4, :]], 0)


def last_step(own_ref, vel_ref, direct_ref, moments_ref, spots_ref, pos_ref, speed_ref, accel_ref, picked_ref):
    for b in range(2):
        for e in range(FAR):
            line = moments_ref[pl.ds(spots_ref[b, e], 1), :]
            picked_ref[b * FAR + e : b * FAR + e + 1, :] = pltpu.roll(line, spots_ref[2 + b, e], 1)
    far = []
    for b in range(2):
        x, y, z = [own_ref[c : c + 1, B * b : B * b + B] for c in range(3)]
        far.append(jnp.concatenate(far_sum(x, y, z, picked_ref[FAR * b : FAR * b + FAR, :]), 0))
    accel = direct_ref[...] + jnp.concatenate(far, 1)
    accel_ref[...] = accel
    speed = vel_ref[...] + timestep * accel
    speed_ref[...] = speed
    pos_ref[...] = own_ref[0:3, :] + (0.5 * timestep) * speed


def exchange(value, axis):
    return lax.all_to_all(value, axis, split_axis=0, concat_axis=0, tiled=True)


def on_device(positions, velocities, masses, near_list, near_count, far_list):
    message = shape(N_GRP, 4, 128)
    direct_scratch = [
        pltpu.VMEM((48, N_SEC * W), bf16),
        pltpu.VMEM((32, N_SEC * W), bf16),
    ]
    pairs = W * N_SEC * W
    direct_cost = pl.CostEstimate(flops=160 * pairs, bytes_accessed=200000, transcendentals=pairs)
    inputs = (positions, velocities, masses.reshape(1, W), far_list, near_list, near_count)
    send, own, times, spots = pl.pallas_call(
        opening,
        out_shape=(
            shape(N_SEC, 1, LINE),
            shape(4, W),
            shape(2, KBLK, 128),
            jax.ShapeDtypeStruct((4, FAR), jnp.int32),
        ),
        in_specs=[pl.BlockSpec(memory_space=pl.ANY)] * 6,
        out_specs=(VMEM,) * 4,
        scratch_shapes=[
            pltpu.VMEM((3, W), f32),
            pltpu.VMEM((3, W), f32),
            pltpu.VMEM((1, W), f32),
            pltpu.VMEM((2, FAR), jnp.int32),
            pltpu.VMEM((2, LIST), jnp.int32),
            pltpu.SMEM((2,), jnp.int32),
            pltpu.VMEM((8, 128), f32),
            pltpu.SemaphoreType.DMA((6,)),
        ],
        compiler_params=PARAMS,
    )(*[pltpu.with_memory_space_constraint(v, pltpu.HBM) for v in inputs])
    ghosts = exchange(send, "sec")
    first = pl.pallas_call(
        group_moments,
        out_shape=message,
        in_specs=[VMEM],
        out_specs=VMEM,
        compiler_params=PARAMS,
    )(ghosts)
    moments = exchange(first, "grp").reshape(N_GRP * 4, 128)
    near, send = pl.pallas_call(
        first_direct,
        out_shape=(shape(3, W), shape(N_SEC, 1, 3 * W)),
        in_specs=[VMEM] * 4,
        out_specs=(VMEM, VMEM),
        scratch_shapes=direct_scratch,
        compiler_params=PARAMS,
        cost_estimate=direct_cost,
    )(own, ghosts, times, velocities)
    starts = exchange(send, "sec")
    far = pl.pallas_call(
        group_far,
        out_shape=shape(3, N_SEC, W),
        in_specs=[VMEM, VMEM],
        out_specs=VMEM,
        scratch_shapes=[pltpu.VMEM((N_GRP * 4, N_SEC * 128), bf16)],
        compiler_params=PARAMS,
        cost_estimate=pl.CostEstimate(flops=10**10, bytes_accessed=200000, transcendentals=10**6),
    )(ghosts, moments)
    second, halves, own, speed = pl.pallas_call(
        second_moments,
        out_shape=(message, shape(3, N_SEC, W), shape(4, W), shape(3, W)),
        in_specs=[VMEM] * 6,
        out_specs=(VMEM,) * 4,
        compiler_params=PARAMS,
    )(starts, far, ghosts, velocities, near, own)
    moments = exchange(second, "grp").reshape(N_GRP * 4, 128)
    near = pl.pallas_call(
        last_direct,
        out_shape=shape(3, W),
        in_specs=[VMEM] * 4,
        out_specs=VMEM,
        scratch_shapes=direct_scratch,
        compiler_params=PARAMS,
        cost_estimate=direct_cost,
    )(own, ghosts, halves, times)
    return pl.pallas_call(
        last_step,
        out_shape=(shape(3, W),) * 3,
        in_specs=[VMEM, VMEM, VMEM, VMEM, SMEM],
        out_specs=(VMEM,) * 3,
        scratch_shapes=[pltpu.VMEM((2 * FAR, 128), f32)],
        compiler_params=PARAMS,
    )(own, speed, near, moments, spots)


def solution(mesh):
    every = ("sec", "grp")
    placed = (P(None, every), P(None, every), P(every), P(every, None), P(every), P(every, None))
    return jax.shard_map(
        on_device,
        mesh=mesh,
        in_specs=placed,
        out_specs=(P(None, every),) * 3,
        check_vma=False,
    )
```

```python
import jax
import jax.numpy as jnp
from jax import lax
from jax.experimental import pallas as pl
from jax.experimental.pallas import tpu as pltpu
from jax.sharding import PartitionSpec as P

timestep = 0.05
softening = 0.25
N_SEC = 16
N_GRP = 48
B = 256
W = 2 * B
KBLK = 2 * N_SEC
LIST = 64
FAR = 32
CHUNK = 1024
LINE = 4 * W + 128
ORDER = [
    29, 30, 6, 9, 2, 15, 5, 32, 28, 17, 7, 13, 21, 8, 12, 37,
    0, 24, 1, 36, 19, 39, 25, 31, 38, 18, 16, 20, 42, 27, 34, 3,
    14, 43, 26, 41, 4, 33, 44, 46, 47, 22, 10, 11, 45, 40, 23, 35,
]
f32 = jnp.float32
bf16 = jnp.bfloat16
VMEM = pl.BlockSpec(memory_space=pltpu.VMEM)
SMEM = pl.BlockSpec(memory_space=pltpu.SMEM)
PARAMS = pltpu.CompilerParams(vmem_limit_bytes=40 * 1024 * 1024)


def shape(*dims):
    return jax.ShapeDtypeStruct(dims, f32)


def split3(value):
    first = value.astype(bf16).astype(f32)
    rest = value - first
    second = rest.astype(bf16).astype(f32)
    return first, second, rest - second


def opening(
    pos_hbm, vel_hbm, mass_hbm, far_hbm, near_hbm, count_hbm, send_ref, own_ref, times_ref, spots_ref,
    pos_ref, vel_ref, mass_ref, far_ref, near_ref, count_ref, lists_ref, sems,
):
    pairs = (
        (pos_hbm, pos_ref),
        (vel_hbm, vel_ref),
        (mass_hbm, mass_ref),
        (far_hbm, far_ref),
        (near_hbm, near_ref),
        (count_hbm, count_ref),
    )
    copies = [pltpu.make_async_copy(source, target, sems.at[i]) for i, (source, target) in enumerate(pairs)]
    for copy in copies:
        copy.start()
    lists_ref[...] = jnp.zeros_like(lists_ref)
    for copy in copies:
        copy.wait()
    lists_ref[0:2, 0:FAR] = far_ref[...].astype(f32)
    lists = lists_ref[0:1, :] + pltpu.roll(lists_ref[1:2, :], FAR, 1)
    half = pos_ref[...] + (0.5 * timestep) * vel_ref[...]
    own_ref[...] = jnp.concatenate([half, mass_ref[...]], 0)
    line = jnp.concatenate([half[0:1], half[1:2], half[2:3], mass_ref[...], lists], 1)
    for d in range(N_SEC):
        send_ref[d] = line
    row, which = place_of(far_ref[...])
    spots_ref[0:2, :] = row
    spots_ref[2:4, :] = (128 - which * 16) & 127
    block = lax.broadcasted_iota(jnp.int32, (KBLK, LIST), 0)
    slot = lax.broadcasted_iota(jnp.int32, (KBLK, LIST), 1)
    for b in range(2):
        hit = (near_ref[b : b + 1, :] == block) & (slot < count_ref[b])
        times = jnp.sum(jnp.where(hit, 1.0, 0.0).astype(f32), axis=1, keepdims=True)
        times_ref[b] = jnp.broadcast_to(times, (KBLK, 128))


def moments_message(whole):
    section = lax.broadcasted_iota(jnp.int32, (N_SEC, 128), 0)
    lane = lax.broadcasted_iota(jnp.int32, (N_SEC, 128), 1)
    base = section // 4 * 32
    packed = jnp.zeros((N_SEC, 128), f32)

    def total(v):
        return jnp.sum(v, axis=1, keepdims=True)

    for place in range(2):
        x, y, z, m = [w[:, B * place : B * place + B] for w in whole]
        mass = total(m)
        centre = [total(m * v) / mass for v in (x, y, z)]
        dx, dy, dz = [v - c for v, c in zip((x, y, z), centre)]
        radius = dx * dx + dy * dy + dz * dz
        m3 = 3.0 * m
        numbers = [
            mass,
            *centre,
            total(m * (3.0 * dx * dx - radius)),
            total(m * (3.0 * dy * dy - radius)),
            total(m * (3.0 * dz * dz - radius)),
            total(m3 * dx * dy),
            total(m3 * dx * dz),
            total(m3 * dy * dz),
        ]
        for c, number in enumerate(numbers):
            packed = jnp.where(lane == base + (16 * place + c), number, packed)
    return packed[0:4] + packed[4:8] + packed[8:12] + packed[12:16]


def group_moments(ghost_ref, out_ref):
    message = moments_message([ghost_ref[:, 0, W * c : W * c + W] for c in range(4)])
    for k in range(N_GRP):
        out_ref[k] = message


def direct(own_ref, times_ref, fetch, source_ref, weight_ref):
    middle = jnp.sum(own_ref[0:3, :], axis=1, keepdims=True) * (1.0 / W)
    target = own_ref[0:3, :] - middle
    norm = jnp.sum(target * target, axis=0, keepdims=True) + softening
    pad = jnp.zeros((3, W), f32)
    a, b, c = split3(jnp.concatenate([-2.0 * target, jnp.ones((1, W), f32), norm, pad], 0))
    targets = jnp.concatenate([a, a, a, b, b, c], 0).astype(bf16)
    for d in range(N_SEC):
        ghost = fetch(d)
        source = ghost[0:3] - middle
        mass = ghost[3:4]
        square = jnp.sum(source * source, axis=0, keepdims=True)
        a, b, c = split3(jnp.concatenate([source, square, jnp.ones((1, W), f32), pad], 0))
        source_ref[:, W * d : W * d + W] = jnp.concatenate([a, b, c, a, b, a], 0).astype(bf16)
        terms = jnp.concatenate([mass, source * mass], 0)
        k = 2 * d
        both = []
        for t in range(2):
            first, second = times_ref[t, k : k + 1, :], times_ref[t, k + 1 : k + 2, :]
            both.append(terms * jnp.concatenate([first, first, second, second], 1))
        a, b, c = split3(jnp.concatenate(both, 0))
        weight_ref[:, W * d : W * d + W] = jnp.concatenate([a, b, c, jnp.zeros_like(a)], 0).astype(bf16)
    total = jnp.zeros((32, W), f32)
    for start in range(0, N_SEC * W, CHUNK):
        square = lax.dot_general(
            source_ref[:, start : start + CHUNK],
            targets,
            (((0,), (0,)), ((), ())),
            preferred_element_type=f32,
        )
        inverse = lax.rsqrt(square)
        cube = inverse * inverse * inverse
        high = cube.astype(bf16)
        low = (cube - high.astype(f32)).astype(bf16)
        weight = weight_ref[:, start : start + CHUNK]
        total = total + jnp.dot(
            jnp.concatenate([weight, weight], 1), jnp.concatenate([high, low], 0), preferred_element_type=f32
        )
    sums = total[0:8] + total[8:16] + total[16:24]
    lane = lax.broadcasted_iota(jnp.int32, (4, W), 1)
    sums = jnp.where(lane < B, sums[0:4], sums[4:8])
    return sums[1:4] - target * sums[0:1]


def first_direct(own_ref, ghost_ref, times_ref, vel_ref, out_ref, send_ref, *scratch):
    def fetch(d):
        return jnp.concatenate([ghost_ref[d, :, W * c : W * c + W] for c in range(4)], 0)

    near = direct(own_ref, times_ref, fetch, *scratch)
    out_ref[...] = near
    start = own_ref[0:3, :] + timestep * (vel_ref[...] + timestep * near)
    line = jnp.concatenate([start[0:1], start[1:2], start[2:3]], 1)
    for d in range(N_SEC):
        send_ref[d] = line


def last_direct(own_ref, ghost_ref, half_ref, times_ref, out_ref, *scratch):
    def fetch(d):
        rows = [half_ref[c, d : d + 1, :] for c in range(3)]
        return jnp.concatenate([*rows, ghost_ref[d, :, 3 * W : 4 * W]], 0)

    out_ref[...] = direct(own_ref, times_ref, fetch, *scratch)


def place_of(block):
    device = block >> 1
    section = (device * 1366) >> 16
    group = device - section * N_GRP
    member = jnp.zeros_like(group)
    for position, number in enumerate(ORDER):
        member = jnp.where(group == number, position, member)
    return member * 4 + (section & 3), (section >> 2) * 2 + (block & 1)


def far_sum(x, y, z, picked):
    mass, cx, cy, cz, qxx, qyy, qzz, qxy, qxz, qyz = [picked[:, c : c + 1] for c in range(10)]
    x, y, z = x - cx, y - cy, z - cz
    square = x * x + y * y + z * z + softening
    inverse = lax.rsqrt(square)
    two = inverse * inverse
    five = two * two * inverse
    quad_x = qxx * x + qxy * y + qxz * z
    quad_y = qxy * x + qyy * y + qyz * z
    quad_z = qxz * x + qyz * y + qzz * z
    along = 2.5 * (x * quad_x + y * quad_y + z * quad_z) * two - mass * square
    return [
        jnp.sum((along * r - quad) * five, axis=0, keepdims=True)
        for r, quad in ((x, quad_x), (y, quad_y), (z, quad_z))
    ]


def group_far(ghost_ref, moments_ref, out_ref, hot_ref):
    entries = ghost_ref[:, 0, 4 * W : LINE].astype(jnp.int32)
    row, which = place_of(entries)
    rows = N_GRP * 4
    number = lax.broadcasted_iota(jnp.int32, (rows, 128), 0)
    for d in range(N_SEC):
        hot_ref[:, 128 * d : 128 * d + 128] = jnp.where(number == row[d : d + 1, :], 1.0, 0.0).astype(bf16)
    hot = hot_ref[...]
    picked = sum(
        lax.dot_general(part.astype(bf16), hot, (((0,), (0,)), ((), ())), preferred_element_type=f32)
        for part in split3(moments_ref[...])
    )
    for d in range(N_SEC):
        lines = picked[:, 128 * d : 128 * d + 128]
        mine = lines[0:16]
        for k in range(1, 8):
            mine = jnp.where(which[d : d + 1, :] == k, lines[16 * k : 16 * k + 16], mine)
        mine = mine.T
        for place in range(2):
            at = B * place
            x, y, z = [ghost_ref[d, :, W * c + at : W * c + at + B] for c in range(3)]
            parts = far_sum(x, y, z, mine[FAR * place : FAR * place + FAR])
            for c in range(3):
                out_ref[c, d : d + 1, at : at + B] = parts[c]


def second_moments(start_ref, far_ref, ghost_ref, vel_ref, near_ref, own_ref, out_ref, half_ref, next_ref, speed_ref):
    whole = []
    for c in range(3):
        half = start_ref[:, 0, W * c : W * c + W] + (timestep * timestep) * far_ref[c]
        half_ref[c] = half
        whole.append(half)
    message = moments_message([*whole, ghost_ref[:, 0, 3 * W : 4 * W]])
    for k in range(N_GRP):
        out_ref[k] = message
    section = lax.axis_index("sec")
    far = jnp.concatenate([far_ref[c, pl.ds(section, 1), :] for c in range(3)], 0)
    speed = vel_ref[...] + timestep * (near_ref[...] + far)
    speed_ref[...] = speed
    next_ref[...] = jnp.concatenate([own_ref[0:3, :] + timestep * speed, own_ref[3:4, :]], 0)


def last_step(own_ref, vel_ref, direct_ref, moments_ref, spots_ref, pos_ref, speed_ref, accel_ref, picked_ref):
    for b in range(2):
        for e in range(FAR):
            line = moments_ref[pl.ds(spots_ref[b, e], 1), :]
            picked_ref[b * FAR + e : b * FAR + e + 1, :] = pltpu.roll(line, spots_ref[2 + b, e], 1)
    far = []
    for b in range(2):
        x, y, z = [own_ref[c : c + 1, B * b : B * b + B] for c in range(3)]
        far.append(jnp.concatenate(far_sum(x, y, z, picked_ref[FAR * b : FAR * b + FAR, :]), 0))
    accel = direct_ref[...] + jnp.concatenate(far, 1)
    accel_ref[...] = accel
    speed = vel_ref[...] + timestep * accel
    speed_ref[...] = speed
    pos_ref[...] = own_ref[0:3, :] + (0.5 * timestep) * speed


def exchange(value, axis):
    members = [ORDER] if axis == "grp" else None
    return lax.all_to_all(value, axis, split_axis=0, concat_axis=0, tiled=True, axis_index_groups=members)


def on_device(positions, velocities, masses, near_list, near_count, far_list):
    message = shape(N_GRP, 4, 128)
    direct_scratch = [
        pltpu.VMEM((48, N_SEC * W), bf16),
        pltpu.VMEM((32, N_SEC * W), bf16),
    ]
    pairs = W * N_SEC * W
    direct_cost = pl.CostEstimate(flops=160 * pairs, bytes_accessed=200000, transcendentals=pairs)
    inputs = (positions, velocities, masses.reshape(1, W), far_list, near_list, near_count)
    send, own, times, spots = pl.pallas_call(
        opening,
        out_shape=(
            shape(N_SEC, 1, LINE),
            shape(4, W),
            shape(2, KBLK, 128),
            jax.ShapeDtypeStruct((4, FAR), jnp.int32),
        ),
        in_specs=[pl.BlockSpec(memory_space=pl.ANY)] * 6,
        out_specs=(VMEM,) * 4,
        scratch_shapes=[
            pltpu.VMEM((3, W), f32),
            pltpu.VMEM((3, W), f32),
            pltpu.VMEM((1, W), f32),
            pltpu.VMEM((2, FAR), jnp.int32),
            pltpu.VMEM((2, LIST), jnp.int32),
            pltpu.SMEM((2,), jnp.int32),
            pltpu.VMEM((8, 128), f32),
            pltpu.SemaphoreType.DMA((6,)),
        ],
        compiler_params=PARAMS,
    )(*[pltpu.with_memory_space_constraint(v, pltpu.HBM) for v in inputs])
    ghosts = exchange(send, "sec")
    first = pl.pallas_call(
        group_moments,
        out_shape=message,
        in_specs=[VMEM],
        out_specs=VMEM,
        compiler_params=PARAMS,
    )(ghosts)
    moments = exchange(first, "grp").reshape(N_GRP * 4, 128)
    near, send = pl.pallas_call(
        first_direct,
        out_shape=(shape(3, W), shape(N_SEC, 1, 3 * W)),
        in_specs=[VMEM] * 4,
        out_specs=(VMEM, VMEM),
        scratch_shapes=direct_scratch,
        compiler_params=PARAMS,
        cost_estimate=direct_cost,
    )(own, ghosts, times, velocities)
    starts = exchange(send, "sec")
    far = pl.pallas_call(
        group_far,
        out_shape=shape(3, N_SEC, W),
        in_specs=[VMEM, VMEM],
        out_specs=VMEM,
        scratch_shapes=[pltpu.VMEM((N_GRP * 4, N_SEC * 128), bf16)],
        compiler_params=PARAMS,
        cost_estimate=pl.CostEstimate(flops=10**10, bytes_accessed=200000, transcendentals=10**6),
    )(ghosts, moments)
    second, halves, own, speed = pl.pallas_call(
        second_moments,
        out_shape=(message, shape(3, N_SEC, W), shape(4, W), shape(3, W)),
        in_specs=[VMEM] * 6,
        out_specs=(VMEM,) * 4,
        compiler_params=PARAMS,
    )(starts, far, ghosts, velocities, near, own)
    moments = exchange(second, "grp").reshape(N_GRP * 4, 128)
    near = pl.pallas_call(
        last_direct,
        out_shape=shape(3, W),
        in_specs=[VMEM] * 4,
        out_specs=VMEM,
        scratch_shapes=direct_scratch,
        compiler_params=PARAMS,
        cost_estimate=direct_cost,
    )(own, ghosts, halves, times)
    return pl.pallas_call(
        last_step,
        out_shape=(shape(3, W),) * 3,
        in_specs=[VMEM, VMEM, VMEM, VMEM, SMEM],
        out_specs=(VMEM,) * 3,
        scratch_shapes=[pltpu.VMEM((2 * FAR, 128), f32)],
        compiler_params=PARAMS,
    )(own, speed, near, moments, spots)


def solution(mesh):
    every = ("sec", "grp")
    placed = (P(None, every), P(None, every), P(every), P(every, None), P(every), P(every, None))
    return jax.shard_map(
        on_device,
        mesh=mesh,
        in_specs=placed,
        out_specs=(P(None, every),) * 3,
        check_vma=False,
    )
```
